512 devices in a mesh: shot: 8 (over x, z_hi), dom: 64 (over y, z_lo, core).
Axes of the slice: x: 4, y: 8, z: 8 (z_hi: 2, z_lo: 4; z = z_hi * 4 + z_lo), core: 2. Of those that a mesh axis runs over, the one named last changes fastest.
Arguments:
- source_prev: float32 [8, 256, 64, 128], P('shot', 'dom'), may hold values from -6 to 6
- source_now: float32 [8, 256, 64, 128], P('shot', 'dom'), may hold values from -6 to 6
- adjoint_prev: float32 [8, 256, 64, 128], P('shot', 'dom'), may hold values from -6 to 6
- adjoint_now: float32 [8, 256, 64, 128], P('shot', 'dom'), may hold values from -6 to 6
- squared_courant: float32 [256, 64, 256], P('dom', 'shot'), may hold values from 0.03 to 0.15
- offsets: int32 [8], P('shot'), may hold values from 0 to 128, as said below
- traces: float32 [8, 8, 8192], P('shot', None, 'dom'), may hold values from -6 to 6
- receiver_cells: int32 [8, 1, 8192], P('shot', None, 'dom'), may hold values from 0 to 32767
- counts: int32 [8, 64, 64], P('shot', 'dom'), may hold values from 0 to 2, as said below
Outputs:
- source_field: float32 [8, 256, 64, 128], P('shot', 'dom')
- adjoint_field: float32 [8, 256, 64, 128], P('shot', 'dom')
- gradient: float32 [256, 64, 256], P('dom', 'shot')
The draws below stay inside these ranges and needn't reach their ends.
Inputs may be any that keep to these rules, and one draw needn't show every extreme that they name: `counts`: in every shot, some source device fills all 2 slots for some owner. The shots' offsets are distinct, and one of them is exactly 128.
All inputs are finite; a program needn't handle non-finite values.
Results may differ from the reference program's by a relative error of at most 0.0003.
Values sent between devices are 32-bit elements; how exact they have to be, the bound alone decides.
A program may use at most 64 MiB of HBM per device.

```python
import math
import jax
import jax.numpy as jnp
from jax import lax

CX = 4
NY = 64
NZ = 128
OFFSET_MAX = 128
STEPS = 8
CAP = 2
SHOTS = 8
NX = 256
NZM = 256
TRACES = 8192
N_DOM = 64


def draw_counts(key, part):
    key = jax.random.fold_in(key, 5)
    base = jax.random.randint(key, (SHOTS, N_DOM, N_DOM), 0, CAP + 1)
    shot_ids = jnp.arange(SHOTS, dtype=jnp.int32)[:, None, None]
    source = jnp.arange(N_DOM, dtype=jnp.int32)[None, :, None]
    owner = jnp.arange(N_DOM, dtype=jnp.int32)[None, None, :]
    busy = (owner < N_DOM // 4).astype(jnp.int32)
    filled = owner == (source + shot_ids) % N_DOM
    return jnp.where(filled, CAP, jnp.minimum(CAP, base + busy)).astype(jnp.int32)


def draw_offsets(key, part):
    key = jax.random.fold_in(key, 9)
    first_key, second_key = jax.random.split(key)
    chosen = jax.random.permutation(first_key, jnp.arange(OFFSET_MAX, dtype=jnp.int32))[:SHOTS - 1]
    joined = jnp.concatenate([chosen, jnp.full((1,), OFFSET_MAX, jnp.int32)])
    return jax.random.permutation(second_key, joined).astype(jnp.int32)


def touch_ends(entries, key, least, top_value):
    place = [jax.random.randint(jax.random.fold_in(key, axis), (), 0, length) for axis, length in enumerate(entries.shape)]
    longest = entries.shape.index(max(entries.shape))
    neighbour = place[:longest] + [(place[longest] + 1) % entries.shape[longest]] + place[longest + 1:]
    return entries.at[tuple(place)].set(least).at[tuple(neighbour)].set(top_value)


def levels(rng, extent, cuts, low, top_value):
    factor_of = 1.0
    for dim, shards_of in cuts:
        draws = jax.random.uniform(jax.random.fold_in(jax.random.fold_in(rng, 6), dim), (shards_of,), jnp.float32, low / len(cuts), top_value / len(cuts))
        factor_of = factor_of * jnp.repeat(jnp.exp(draws), extent[dim] // shards_of).reshape((-1,) + (1,) * (len(extent) - 1 - dim))
    return factor_of


def noise(rng, extent, scale, limit, shards=(), kind=jnp.bfloat16):
    result = jax.random.normal(rng, extent, jnp.float32) * scale
    if len(shards) > 0:
        result = levels(rng, extent, shards, -0.22, 0.18) * result
    return jnp.clip(result, min=-limit, max=limit).astype(kind)


def setup_inputs(seed: int = 0) -> dict:
    key_of = jax.random.split(jax.random.key(seed), 10)
    return {
        "source_prev": noise(key_of[0], (SHOTS, NX, NY, NZ), 1.0, 6.0, ((0, 8), (1, 64)), jnp.float32),
        "source_now": noise(key_of[1], (SHOTS, NX, NY, NZ), 1.0, 6.0, ((0, 8), (1, 64)), jnp.float32),
        "adjoint_prev": noise(key_of[2], (SHOTS, NX, NY, NZ), 1.0, 6.0, ((0, 8), (1, 64)), jnp.float32),
        "adjoint_now": noise(key_of[3], (SHOTS, NX, NY, NZ), 1.0, 6.0, ((0, 8), (1, 64)), jnp.float32),
        "squared_courant": jnp.clip(jnp.exp(math.log(0.15) - 1.609438 * jax.random.uniform(key_of[4], (NX, NY, NZM), jnp.float32) ** levels(key_of[4], (NX, NY, NZM), ((0, 64), (1, 8)), -0.2, 0.2)), 0.03, 0.15),
        "offsets": draw_offsets(jax.random.fold_in(key_of[9], 71), 0),
        "traces": noise(key_of[6], (SHOTS, STEPS, TRACES), 1.0, 6.0, ((0, 8), (2, 64)), jnp.float32),
        "receiver_cells": touch_ends(jax.random.randint(key_of[7], (SHOTS, 1, TRACES), 0, CX * NY * NZ), jax.random.fold_in(key_of[7], 1), 0, (CX * NY * NZ) - 1).astype(jnp.int32),
        "counts": draw_counts(jax.random.fold_in(key_of[9], 71), 0),
    }


COEFFS = (-205.0 / 72.0, 8.0 / 5.0, -1.0 / 5.0, 8.0 / 315.0, -1.0 / 560.0)


def laplace(padded):
    size_x = padded.shape[0] - 8
    size_y = padded.shape[1] - 8
    size_z = padded.shape[2] - 8
    center = padded[4:4 + size_x, 4:4 + size_y, 4:4 + size_z]
    total = 3.0 * COEFFS[0] * center
    for reach in range(1, 5):
        pair = padded[4 + reach:4 + reach + size_x, 4:4 + size_y, 4:4 + size_z] + padded[4 - reach:4 - reach + size_x, 4:4 + size_y, 4:4 + size_z]
        pair = pair + padded[4:4 + size_x, 4 + reach:4 + reach + size_y, 4:4 + size_z] + padded[4:4 + size_x, 4 - reach:4 - reach + size_y, 4:4 + size_z]
        pair = pair + padded[4:4 + size_x, 4:4 + size_y, 4 + reach:4 + reach + size_z] + padded[4:4 + size_x, 4:4 + size_y, 4 - reach:4 - reach + size_z]
        total = total + COEFFS[reach] * pair
    return total


def reference(source_prev, source_now, adjoint_prev, adjoint_now, squared_courant, offsets, traces, receiver_cells, counts):
    block_cells = CX * NY * NZ

    def one_shot(summed, inputs):
        src_prev, src_now, adj_prev, adj_now, shot_traces, shot_cells, shot_counts, offset = inputs
        courant = lax.dynamic_slice_in_dim(squared_courant, offset.astype(jnp.int32), NZ, 2)
        live = jnp.arange(CAP, dtype=jnp.int32)[None, None, :] < shot_counts[:, :, None]
        values = jnp.where(live[None], shot_traces.reshape(STEPS, N_DOM, N_DOM, CAP), jnp.float32(0.0)).reshape(STEPS, -1)
        owner = jnp.arange(N_DOM, dtype=jnp.int32)[None, :, None]
        index = (owner * block_cells + shot_cells.reshape(N_DOM, N_DOM, CAP)).reshape(-1).astype(jnp.int32)
        image = jnp.zeros((NX, NY, NZ), jnp.float32)
        for moment in range(STEPS):
            lap_source = laplace(jnp.pad(src_now, 4))
            lap_adjoint = laplace(jnp.pad(adj_now, 4))
            image = image + adj_now * lap_source
            src_next = 2.0 * src_now - src_prev + courant * lap_source
            adj_next = 2.0 * adj_now - adj_prev + courant * lap_adjoint
            adj_next = adj_next.reshape(-1).at[index].add(values[moment]).reshape(NX, NY, NZ)
            src_prev, src_now = src_now, src_next
            adj_prev, adj_now = adj_now, adj_next
        placed = lax.dynamic_update_slice(jnp.zeros((NX, NY, NZM), jnp.float32), image / STEPS, (jnp.int32(0), jnp.int32(0), offset.astype(jnp.int32)))
        return summed + placed, (src_now, adj_now)

    start = jnp.zeros((NX, NY, NZM), jnp.float32)
    gradient, fields = lax.scan(one_shot, start, (source_prev, source_now, adjoint_prev, adjoint_now, traces, receiver_cells, counts, offsets))
    return fields[0], fields[1], gradient
```

```python
import functools

import jax
import jax.numpy as jnp
from jax import lax
from jax.experimental import pallas as pl
from jax.experimental.pallas import tpu as pltpu
from jax.sharding import PartitionSpec as P

STEPS = 8
COEFFS = (-205.0 / 72.0, 8.0 / 5.0, -1.0 / 5.0, 8.0 / 315.0, -1.0 / 560.0)
MESH = pl.DeviceIdType.MESH
ROWS = pl.ds(8, 64)
OWN = pl.ds(4, 4)


def remote(src, dst, send, recv, where):
    return pltpu.make_async_remote_copy(
        src_ref=src, dst_ref=dst, send_sem=send, recv_sem=recv, device_id=where, device_id_type=MESH
    )


def lane_iota(shape):
    return lax.broadcasted_iota(jnp.int32, shape, len(shape) - 1)


def rolled(value, shift):
    return pltpu.roll(value, shift % 128, value.ndim - 1) if shift % 128 else value


def kernel(
    src_prev, src_now, adj_prev, adj_now, model, offsets, traces, cells, counts,
    src_out, adj_out, grad_out,
    x, lap, inj, courant, image, turned, pieces, grads, trace_send, trace_y, trace_row, slots, onehot,
    load_sem, halo_send, halo_recv, ty_send, ty_recv, tr_send, tr_recv, c_send, c_recv, g_send, g_recv,
):
    s = lax.axis_index("shot")
    d = lax.axis_index("dom")
    y, g = d // 8, d % 8
    sx, sz = s // 2, s % 2
    has_left, has_right = d > 0, d < 63
    off = offsets[0]

    loads = [
        pltpu.make_async_copy(ref.at[0], x.at[time, field, OWN, ROWS], load_sem.at[time, field])
        for time, field, ref in ((0, 0, src_now), (0, 1, adj_now), (1, 0, src_prev), (1, 1, adj_prev))
    ]

    for time in range(2):
        for field in range(2):
            for plane in range(12):
                if 4 <= plane < 8:
                    x[time, field, plane, 0:8] = jnp.zeros((8, 128), jnp.float32)
                    x[time, field, plane, 72:80] = jnp.zeros((8, 128), jnp.float32)
                else:
                    x[time, field, plane] = jnp.zeros((80, 128), jnp.float32)
    for copy in loads:
        copy.start()

    barrier = pltpu.get_barrier_semaphore()
    line = [(s, ((y + k) % 8) * 8 + g) for k in range(1, 8)]
    row = [(s, y * 8 + (g + k) % 8) for k in range(1, 8)]
    shot = {}
    for dz in range(2):
        for k in range(4):
            shot[dz, k] = (((sx + k) % 4) * 2 + (sz + dz) % 2, d)
    others = [key for key in shot if key != (0, 0)]
    for where in line + row + [shot[key] for key in others]:
        pl.semaphore_signal(barrier, inc=1, device_id=where, device_id_type=MESH)
    left_far = jnp.logical_and(has_left, g == 0)
    right_far = jnp.logical_and(has_right, g == 7)

    @pl.when(left_far)
    def _():
        pl.semaphore_signal(barrier, inc=1, device_id=(s, d - 1), device_id_type=MESH)

    @pl.when(right_far)
    def _():
        pl.semaphore_signal(barrier, inc=1, device_id=(s, d + 1), device_id_type=MESH)

    for plane in range(4):
        for half in range(2):
            pieces[0, 2 * plane + half] = model[plane, :, 128 * half : 128 * half + 128]
    pieces[0, 8] = jnp.full((8, 128), off, jnp.int32).astype(jnp.float32)
    spread = (lax.broadcasted_iota(jnp.int32, (64, 128), 0) == lane_iota((64, 128)) // 2).astype(jnp.float32)
    filled = jnp.broadcast_to(counts[0].astype(jnp.float32), (8, 64))
    live = (lane_iota((8, 128)) % 2).astype(jnp.float32) < jnp.dot(
        filled, spread, preferred_element_type=jnp.float32
    ) - 0.5
    trace_send[0:8] = jnp.where(live, traces[0], 0.0)
    trace_send[8:16] = jnp.broadcast_to(cells[0].astype(jnp.float32), (8, 128))

    far = left_far.astype(jnp.int32) + right_far.astype(jnp.int32)
    pl.semaphore_wait(barrier, 21 + far)

    def to_right(time):
        return remote(
            x.at[time, :, OWN, ROWS], x.at[time, :, pl.ds(0, 4), ROWS],
            halo_send.at[time, 0], halo_recv.at[time, 0], (s, d + 1),
        )

    def to_left(time):
        return remote(
            x.at[time, :, OWN, ROWS], x.at[time, :, pl.ds(8, 4), ROWS],
            halo_send.at[time, 1], halo_recv.at[time, 1], (s, d - 1),
        )

    def send_halos(time):
        @pl.when(has_right)
        def _():
            to_right(time).start()

        @pl.when(has_left)
        def _():
            to_left(time).start()

    def sent_halos(time):
        @pl.when(has_right)
        def _():
            to_right(time).wait_send()

        @pl.when(has_left)
        def _():
            to_left(time).wait_send()

    def got_halos(time):
        @pl.when(has_left)
        def _():
            to_right(time).wait_recv()

        @pl.when(has_right)
        def _():
            to_left(time).wait_recv()

    first = [
        remote(trace_send, trace_y.at[k], ty_send.at[k], ty_recv.at[k], line[k - 1]) for k in range(1, 8)
    ]
    for copy in first:
        copy.start()
    spread_1 = [
        remote(pieces.at[0], pieces.at[dz * 4 + k], c_send.at[dz * 4 + k], c_recv.at[dz * 4 + k], shot[dz, k])
        for dz, k in ((1, 0), (0, 1), (0, 2), (0, 3))
    ]
    for copy in spread_1:
        copy.start()
    loads[0].wait()
    loads[1].wait()
    send_halos(0)

    trace_y[0] = trace_send[...]
    for copy in first:
        copy.wait_recv()
    lane = lane_iota((16, 128))
    packed = jnp.zeros((16, 128), jnp.float32)
    for k in range(8):
        packed = packed + jnp.where(lane // 16 == (y + 8 - k) % 8, rolled(trace_y[k], -16 * k), 0.0)
    trace_row[0] = packed
    second = [
        remote(trace_row.at[0], trace_row.at[k], tr_send.at[k], tr_recv.at[k], row[k - 1]) for k in range(1, 8)
    ]
    for copy in second:
        copy.start()
    spread_1[0].wait_recv()
    spread_2 = [
        remote(pieces.at[4], pieces.at[4 + k], c_send.at[4 + k], c_recv.at[4 + k], shot[0, k]) for k in range(1, 4)
    ]
    for copy in spread_2:
        copy.start()
    for copy in second:
        copy.wait_recv()
    own = jnp.zeros((16, 128), jnp.float32)
    for k in range(8):
        own = own + jnp.where((lane // 2) % 8 == (g + 8 - k) % 8, rolled(trace_row[k], -2 * k), 0.0)
    slots[...] = own
    cell = own[8:9].astype(jnp.int32)
    onehot[...] = (
        lax.broadcasted_iota(jnp.int32, (256, 128), 0) == jnp.broadcast_to(cell >> 7, (256, 128))
    ).astype(jnp.float32).astype(jnp.bfloat16)
    for copy in spread_1[1:] + spread_2:
        copy.wait_recv()
    at = lane_iota((8, 128)) < 128 - off
    turn_back = lax.rem(128 - off, 128)
    for dz in range(2):
        for k in range(4):
            j = ((sx + 4 - k) % 4) * 2 + (sz + dz) % 2
            for plane in range(4):
                low = pltpu.roll(pieces[dz * 4 + k, 2 * plane], turn_back, 1)
                high = pltpu.roll(pieces[dz * 4 + k, 2 * plane + 1], turn_back, 1)
                courant[plane, pl.ds(pl.multiple_of(j * 8, 8), 8)] = jnp.where(at, low, high)
    loads[2].wait()
    loads[3].wait()
    for plane in range(4):
        image[plane] = jnp.zeros((64, 128), jnp.float32)

    lanes = lane_iota((64, 128))

    @pl.loop(0, STEPS)
    def _(t):
        now = t % 2
        new = 1 - now
        value = slots[pl.ds(t, 1)]
        cell_lane = slots[8:9].astype(jnp.int32) & 127
        hit = lax.broadcasted_iota(jnp.int32, (128, 128), 0) == jnp.broadcast_to(cell_lane, (128, 128))
        placed = jnp.where(hit, jnp.broadcast_to(value, (128, 128)), 0.0)
        high = placed.astype(jnp.bfloat16)
        low = (placed - high.astype(jnp.float32)).astype(jnp.bfloat16)
        dims = (((1,), (1,)), ((), ()))
        inj[...] = lax.dot_general(
            onehot[...], high, dims, preferred_element_type=jnp.float32
        ) + lax.dot_general(onehot[...], low, dims, preferred_element_type=jnp.float32)
        for field in range(2):
            for plane in range(4):
                center = x[now, field, 4 + plane, ROWS]
                total = 3.0 * COEFFS[0] * center
                for reach in range(1, 5):
                    pair = x[now, field, 4 + plane, pl.ds(8 + reach, 64)] + x[now, field, 4 + plane, pl.ds(8 - reach, 64)]
                    pair = pair + jnp.where(lanes >= reach, rolled(center, reach), 0.0)
                    pair = pair + jnp.where(lanes < 128 - reach, rolled(center, -reach), 0.0)
                    for other in (plane - reach, plane + reach):
                        if 0 <= other < 4:
                            pair = pair + x[now, field, 4 + other, ROWS]
                    total = total + COEFFS[reach] * pair
                lap[field, plane] = total

        @pl.when(t > 0)
        def _():
            sent_halos(new)

        got_halos(now)
        for field in range(2):
            for plane in range(4):
                total = lap[field, plane]
                for reach in range(1, 5):
                    for other in (plane - reach, plane + reach):
                        if not 0 <= other < 4:
                            total = total + COEFFS[reach] * x[now, field, 4 + other, ROWS]
                center = x[now, field, 4 + plane, ROWS]
                following = 2.0 * center - x[new, field, 4 + plane, ROWS] + courant[plane] * total
                if field == 0:
                    image[plane] += x[now, 1, 4 + plane, ROWS] * total
                else:
                    following = following + inj[64 * plane : 64 * plane + 64]
                x[new, field, 4 + plane, ROWS] = following

        @pl.when(t < STEPS - 1)
        def _():
            send_halos(new)

    sent_halos((STEPS - 1) % 2)

    turn = lax.rem(off, 128)
    for plane in range(4):
        turned[plane] = pltpu.roll(image[plane] * (1.0 / STEPS), turn, 1)
    grad_copies = []
    for dz, k in others:
        j = ((sx + k) % 4) * 2 + (sz + dz) % 2
        grad_copies.append(
            remote(
                turned.at[:, pl.ds(pl.multiple_of(j * 8, 8), 8)], grads.at[dz * 4 + k],
                g_send.at[dz * 4 + k], g_recv.at[dz * 4 + k], shot[dz, k],
            )
        )
    for copy in grad_copies:
        copy.start()
    src_out[0] = x[STEPS % 2, 0, OWN, ROWS]
    adj_out[0] = x[STEPS % 2, 1, OWN, ROWS]
    for copy in grad_copies:
        copy.wait_recv()
    lane8 = lane_iota((8, 128)).astype(jnp.float32)
    for plane in range(4):
        mine = turned[plane, pl.ds(pl.multiple_of(s * 8, 8), 8)]
        low = jnp.where(lane8 >= pieces[0, 8], mine, 0.0)
        high = mine - low
        for dz, k in others:
            part = grads[dz * 4 + k, plane]
            start = pieces[dz * 4 + k, 8]
            low = low + jnp.where(lane8 >= start, part, 0.0)
            high = high + jnp.where(lane8 < start, part, 0.0)
        grad_out[plane, :, 0:128] = low
        grad_out[plane, :, 128:256] = high
    for copy in first + second + spread_1 + spread_2 + grad_copies:
        copy.wait_send()


def shards(source_prev, source_now, adjoint_prev, adjoint_now, squared_courant, offsets, traces, receiver_cells, counts):
    field = jax.ShapeDtypeStruct(source_now.shape, jnp.float32)
    any_spec = pl.BlockSpec(memory_space=pl.ANY)
    vmem = pl.BlockSpec(memory_space=pltpu.VMEM)
    f32 = jnp.float32
    return pl.pallas_call(
        kernel,
        out_shape=(field, field, jax.ShapeDtypeStruct(squared_courant.shape, f32)),
        in_specs=[any_spec] * 4 + [vmem, pl.BlockSpec(memory_space=pltpu.SMEM), vmem, vmem, vmem],
        out_specs=(vmem, vmem, vmem),
        scratch_shapes=[
            pltpu.VMEM((2, 2, 12, 80, 128), f32),
            pltpu.VMEM((2, 4, 64, 128), f32),
            pltpu.VMEM((256, 128), f32),
            pltpu.VMEM((4, 64, 128), f32),
            pltpu.VMEM((4, 64, 128), f32),
            pltpu.VMEM((4, 64, 128), f32),
            pltpu.VMEM((8, 9, 8, 128), f32),
            pltpu.VMEM((8, 4, 8, 128), f32),
            pltpu.VMEM((16, 128), f32),
            pltpu.VMEM((8, 16, 128), f32),
            pltpu.VMEM((8, 16, 128), f32),
            pltpu.VMEM((16, 128), f32),
            pltpu.VMEM((256, 128), jnp.bfloat16),
            pltpu.SemaphoreType.DMA((2, 2)),
            pltpu.SemaphoreType.DMA((2, 2)),
            pltpu.SemaphoreType.DMA((2, 2)),
            pltpu.SemaphoreType.DMA((8,)),
            pltpu.SemaphoreType.DMA((8,)),
            pltpu.SemaphoreType.DMA((8,)),
            pltpu.SemaphoreType.DMA((8,)),
            pltpu.SemaphoreType.DMA((8,)),
            pltpu.SemaphoreType.DMA((8,)),
            pltpu.SemaphoreType.DMA((8,)),
            pltpu.SemaphoreType.DMA((8,)),
        ],
        compiler_params=pltpu.CompilerParams(
            collective_id=0, has_side_effects=True, vmem_limit_bytes=40 * 1024 * 1024
        ),
    )(source_prev, source_now, adjoint_prev, adjoint_now, squared_courant, offsets, traces, receiver_cells, counts)


def solution(mesh):
    placed = (
        P("shot", "dom", None, None),
        P("shot", "dom", None, None),
        P("shot", "dom", None, None),
        P("shot", "dom", None, None),
        P("dom", "shot", None),
        P("shot"),
        P("shot", None, "dom"),
        P("shot", None, "dom"),
        P("shot", "dom", None),
    )
    return jax.shard_map(
        shards,
        mesh=mesh,
        in_specs=placed,
        out_specs=(
            P("shot", "dom", None, None),
            P("shot", "dom", None, None),
            P("dom", "shot", None),
        ),
        check_vma=False,
    )
```

```python
import functools

import jax
import jax.numpy as jnp
from jax import lax
from jax.experimental import pallas as pl
from jax.experimental.pallas import tpu as pltpu
from jax.sharding import PartitionSpec as P

STEPS = 8
COEFFS = (-205.0 / 72.0, 8.0 / 5.0, -1.0 / 5.0, 8.0 / 315.0, -1.0 / 560.0)
MESH = pl.DeviceIdType.MESH
ROWS = pl.ds(8, 64)
OWN = pl.ds(4, 4)


def remote(src, dst, send, recv, where):
    return pltpu.make_async_remote_copy(
        src_ref=src, dst_ref=dst, send_sem=send, recv_sem=recv, device_id=where, device_id_type=MESH
    )


def lane_iota(shape):
    return lax.broadcasted_iota(jnp.int32, shape, len(shape) - 1)


def rolled(value, shift):
    return pltpu.roll(value, shift % 128, value.ndim - 1) if shift % 128 else value


def kernel(
    src_prev, src_now, adj_prev, adj_now, model_in, offsets_in, traces_in, cells_in, counts_in,
    src_out, adj_out, grad_out,
    x, lap, inj, courant, image, turned, pieces, grads, trace_send, trace_y, trace_row, slots, onehot,
    traces, cells, counts, offsets, summed,
    load_sem, small_sem, halo_send, halo_recv, ty_send, ty_recv, tr_send, tr_recv, c_send, c_recv, g_send, g_recv,
):
    s = lax.axis_index("shot")
    d = lax.axis_index("dom")
    y, g = d // 8, d % 8
    sx, sz = s // 2, s % 2
    has_left, has_right = d > 0, d < 63

    loads = [
        pltpu.make_async_copy(ref.at[0], x.at[time, field, OWN, ROWS], load_sem.at[time, field])
        for time, field, ref in ((0, 0, src_now), (0, 1, adj_now), (1, 0, src_prev), (1, 1, adj_prev))
    ]

    halves = [
        pltpu.make_async_copy(
            model_in.at[:, :, pl.ds(128 * half, 128)], pieces.at[0, pl.ds(4 * half, 4)], small_sem.at[half]
        )
        for half in range(2)
    ]
    small = [
        pltpu.make_async_copy(ref.at[0], scratch, small_sem.at[2 + i])
        for i, (ref, scratch) in enumerate(((traces_in, traces), (cells_in, cells), (counts_in, counts)))
    ] + [pltpu.make_async_copy(offsets_in, offsets, small_sem.at[5])]
    barrier = pltpu.get_barrier_semaphore()
    line = [(s, ((y + k) % 8) * 8 + g) for k in range(1, 8)]
    row = [(s, y * 8 + (g + k) % 8) for k in range(1, 8)]
    shot = {}
    for dz in range(2):
        for k in range(4):
            shot[dz, k] = (((sx + k) % 4) * 2 + (sz + dz) % 2, d)
    others = [key for key in shot if key != (0, 0)]
    for where in line + row + [shot[key] for key in others]:
        pl.semaphore_signal(barrier, inc=1, device_id=where, device_id_type=MESH)
    left_far = jnp.logical_and(has_left, g == 0)
    right_far = jnp.logical_and(has_right, g == 7)

    @pl.when(left_far)
    def _():
        pl.semaphore_signal(barrier, inc=1, device_id=(s, d - 1), device_id_type=MESH)

    @pl.when(right_far)
    def _():
        pl.semaphore_signal(barrier, inc=1, device_id=(s, d + 1), device_id_type=MESH)

    for copy in small + halves + loads:
        copy.start()

    for time in range(2):
        for field in range(2):
            for plane in range(4, 8):
                x[time, field, plane, 0:8] = jnp.zeros((8, 128), jnp.float32)
                x[time, field, plane, 72:80] = jnp.zeros((8, 128), jnp.float32)

    def clear(first_plane):
        for time in range(2):
            for field in range(2):
                for plane in range(first_plane, first_plane + 4):
                    x[time, field, plane, ROWS] = jnp.zeros((64, 128), jnp.float32)

    @pl.when(jnp.logical_not(has_left))
    def _():
        clear(0)

    @pl.when(jnp.logical_not(has_right))
    def _():
        clear(8)

    for copy in small:
        copy.wait()
    off = offsets[0]
    pieces[0, 8] = jnp.full((8, 128), off, jnp.int32).astype(jnp.float32)
    spread = (lax.broadcasted_iota(jnp.int32, (64, 128), 0) == lane_iota((64, 128)) // 2).astype(jnp.float32)
    filled = jnp.broadcast_to(counts[...].astype(jnp.float32), (8, 64))
    live = (lane_iota((8, 128)) % 2).astype(jnp.float32) < jnp.dot(
        filled, spread, preferred_element_type=jnp.float32
    ) - 0.5
    trace_send[0:8] = jnp.where(live, traces[...], 0.0)
    trace_send[8:16] = jnp.broadcast_to(cells[...].astype(jnp.float32), (8, 128))

    far = left_far.astype(jnp.int32) + right_far.astype(jnp.int32)
    pl.semaphore_wait(barrier, 21 + far)

    def to_right(time, field):
        return remote(
            x.at[time, field, OWN, ROWS], x.at[time, field, pl.ds(0, 4), ROWS],
            halo_send.at[time, 0, field], halo_recv.at[time, 0, field], (s, d + 1),
        )

    def to_left(time, field):
        return remote(
            x.at[time, field, OWN, ROWS], x.at[time, field, pl.ds(8, 4), ROWS],
            halo_send.at[time, 1, field], halo_recv.at[time, 1, field], (s, d - 1),
        )

    def send_halos(time, field):
        @pl.when(has_right)
        def _():
            to_right(time, field).start()

        @pl.when(has_left)
        def _():
            to_left(time, field).start()

    def sent_halos(time, field):
        @pl.when(has_right)
        def _():
            to_right(time, field).wait_send()

        @pl.when(has_left)
        def _():
            to_left(time, field).wait_send()

    def got_halos(time, field):
        @pl.when(has_left)
        def _():
            to_right(time, field).wait_recv()

        @pl.when(has_right)
        def _():
            to_left(time, field).wait_recv()

    lanes = lane_iota((64, 128))

    def inside(time, field):
        for plane in range(4):
            center = x[time, field, 4 + plane, ROWS]
            total = 3.0 * COEFFS[0] * center
            for reach in range(1, 5):
                pair = x[time, field, 4 + plane, pl.ds(8 + reach, 64)] + x[time, field, 4 + plane, pl.ds(8 - reach, 64)]
                pair = pair + jnp.where(lanes >= reach, rolled(center, reach), 0.0)
                pair = pair + jnp.where(lanes < 128 - reach, rolled(center, -reach), 0.0)
                for other in (plane - reach, plane + reach):
                    if 0 <= other < 4:
                        pair = pair + x[time, field, 4 + other, ROWS]
                total = total + COEFFS[reach] * pair
            lap[field, plane] = total

    def injection(t):
        value = slots[pl.ds(t, 1)]
        cell_lane = slots[8:9].astype(jnp.int32) & 127
        hit = lax.broadcasted_iota(jnp.int32, (128, 128), 0) == jnp.broadcast_to(cell_lane, (128, 128))
        placed = jnp.where(hit, jnp.broadcast_to(value, (128, 128)), 0.0)
        high = placed.astype(jnp.bfloat16)
        low = (placed - high.astype(jnp.float32)).astype(jnp.bfloat16)
        dims = (((1,), (1,)), ((), ()))
        inj[...] = lax.dot_general(
            onehot[...], high, dims, preferred_element_type=jnp.float32
        ) + lax.dot_general(onehot[...], low, dims, preferred_element_type=jnp.float32)

    def advance(now, new, field):
        for plane in range(4):
            total = lap[field, plane]
            for reach in range(1, 5):
                for other in (plane - reach, plane + reach):
                    if not 0 <= other < 4:
                        total = total + COEFFS[reach] * x[now, field, 4 + other, ROWS]
            center = x[now, field, 4 + plane, ROWS]
            following = 2.0 * center - x[new, field, 4 + plane, ROWS] + courant[plane] * total
            if field == 0:
                image[plane] += x[now, 1, 4 + plane, ROWS] * total
            else:
                following = following + inj[64 * plane : 64 * plane + 64]
            x[new, field, 4 + plane, ROWS] = following

    spread_1 = [
        remote(pieces.at[0], pieces.at[dz * 4 + k], c_send.at[dz * 4 + k], c_recv.at[dz * 4 + k], shot[dz, k])
        for dz, k in ((1, 0), (0, 1), (0, 2), (0, 3))
    ]
    for copy in halves:
        copy.wait()
    for copy in spread_1:
        copy.start()
    loads[0].wait()
    send_halos(0, 0)
    first = [
        remote(trace_send, trace_y.at[k], ty_send.at[k], ty_recv.at[k], line[k - 1]) for k in range(1, 8)
    ]
    for copy in first:
        copy.start()
    loads[1].wait()
    send_halos(0, 1)
    inside(0, 0)

    trace_y[0] = trace_send[...]
    spread_1[0].wait_recv()
    spread_2 = [
        remote(pieces.at[4], pieces.at[4 + k], c_send.at[4 + k], c_recv.at[4 + k], shot[0, k]) for k in range(1, 4)
    ]
    for copy in spread_2:
        copy.start()
    for copy in first:
        copy.wait_recv()
    lane = lane_iota((16, 128))
    packed = jnp.zeros((16, 128), jnp.float32)
    for k in range(8):
        packed = packed + jnp.where(lane // 16 == (y + 8 - k) % 8, rolled(trace_y[k], -16 * k), 0.0)
    trace_row[0] = packed
    along = [
        remote(trace_row.at[0], trace_row.at[k], tr_send.at[k], tr_recv.at[k], row[k - 1]) for k in range(1, 8)
    ]
    for copy in along:
        copy.start()
    inside(0, 1)
    for copy in spread_1[1:] + spread_2:
        copy.wait_recv()
    at = lane_iota((8, 128)) < 128 - off
    turn_back = lax.rem(128 - off, 128)
    for dz in range(2):
        for k in range(4):
            j = ((sx + 4 - k) % 4) * 2 + (sz + dz) % 2
            for plane in range(4):
                low = pltpu.roll(pieces[dz * 4 + k, plane], turn_back, 1)
                high = pltpu.roll(pieces[dz * 4 + k, 4 + plane], turn_back, 1)
                courant[plane, pl.ds(pl.multiple_of(j * 8, 8), 8)] = jnp.where(at, low, high)
    loads[2].wait()
    loads[3].wait()
    for plane in range(4):
        image[plane] = jnp.zeros((64, 128), jnp.float32)

    got_halos(0, 0)
    advance(0, 1, 0)
    send_halos(1, 0)
    inside(1, 0)
    for copy in along:
        copy.wait_recv()
    own = jnp.zeros((16, 128), jnp.float32)
    for k in range(8):
        own = own + jnp.where((lane // 2) % 8 == (g + 8 - k) % 8, rolled(trace_row[k], -2 * k), 0.0)
    slots[...] = own
    cell = own[8:9].astype(jnp.int32)
    onehot[...] = (
        lax.broadcasted_iota(jnp.int32, (256, 128), 0) == jnp.broadcast_to(cell >> 7, (256, 128))
    ).astype(jnp.float32).astype(jnp.bfloat16)
    injection(0)
    got_halos(0, 1)
    advance(0, 1, 1)
    send_halos(1, 1)
    inside(1, 1)
    injection(1)

    @pl.loop(1, STEPS - 1)
    def _(t):
        now = t % 2
        new = 1 - now
        for field in range(2):
            sent_halos(new, field)
            got_halos(now, field)
            advance(now, new, field)
            send_halos(new, field)
            inside(new, field)
        injection(t + 1)

    now = (STEPS - 1) % 2
    new = 1 - now
    results = [
        pltpu.make_async_copy(x.at[new, field, OWN, ROWS], ref.at[0], small_sem.at[field])
        for field, ref in enumerate((src_out, adj_out))
    ]
    sent_halos(new, 0)
    got_halos(now, 0)
    advance(now, new, 0)

    turn = lax.rem(off, 128)
    for plane in range(4):
        turned[plane] = pltpu.roll(image[plane] * (1.0 / STEPS), turn, 1)
    grad_copies = []
    for dz, k in others:
        j = ((sx + k) % 4) * 2 + (sz + dz) % 2
        grad_copies.append(
            remote(
                turned.at[:, pl.ds(pl.multiple_of(j * 8, 8), 8)], grads.at[dz * 4 + k],
                g_send.at[dz * 4 + k], g_recv.at[dz * 4 + k], shot[dz, k],
            )
        )
    for copy in grad_copies:
        copy.start()
    results[0].start()
    sent_halos(new, 1)
    got_halos(now, 1)
    advance(now, new, 1)
    results[1].start()
    for copy in grad_copies:
        copy.wait_recv()
    lane8 = lane_iota((8, 128)).astype(jnp.float32)
    for plane in range(4):
        mine = turned[plane, pl.ds(pl.multiple_of(s * 8, 8), 8)]
        low = jnp.where(lane8 >= pieces[0, 8], mine, 0.0)
        high = mine - low
        for dz, k in others:
            part = grads[dz * 4 + k, plane]
            start = pieces[dz * 4 + k, 8]
            low = low + jnp.where(lane8 >= start, part, 0.0)
            high = high + jnp.where(lane8 < start, part, 0.0)
        summed[plane, :, 0:128] = low
        summed[plane, :, 128:256] = high
    gradient = pltpu.make_async_copy(summed, grad_out, small_sem.at[2])
    gradient.start()
    for copy in first + along + spread_1 + spread_2 + grad_copies:
        copy.wait_send()
    for field in range(2):
        sent_halos(now, field)
    for copy in results + [gradient]:
        copy.wait()


def deliver(*refs):
    given, wanted, held, sems = refs[0:3], refs[3:6], refs[6:9], refs[9]
    into = [pltpu.make_async_copy(a, b, sems.at[0, i]) for i, (a, b) in enumerate(zip(given, held, strict=True))]
    out = [pltpu.make_async_copy(a, b, sems.at[1, i]) for i, (a, b) in enumerate(zip(held, wanted, strict=True))]
    for copy in into:
        copy.start()
    for i in range(3):
        into[i].wait()
        out[i].start()
    for copy in out:
        copy.wait()


def shards(source_prev, source_now, adjoint_prev, adjoint_now, squared_courant, offsets, traces, receiver_cells, counts):
    field = jax.ShapeDtypeStruct(source_now.shape, jnp.float32)
    hbm = pl.BlockSpec(memory_space=pltpu.HBM)
    f32 = jnp.float32
    results = pl.pallas_call(
        kernel,
        out_shape=(field, field, jax.ShapeDtypeStruct(squared_courant.shape, f32)),
        in_specs=[hbm] * 9,
        out_specs=(hbm, hbm, hbm),
        scratch_shapes=[
            pltpu.VMEM((2, 2, 12, 80, 128), f32),
            pltpu.VMEM((2, 4, 64, 128), f32),
            pltpu.VMEM((256, 128), f32),
            pltpu.VMEM((4, 64, 128), f32),
            pltpu.VMEM((4, 64, 128), f32),
            pltpu.VMEM((4, 64, 128), f32),
            pltpu.VMEM((8, 9, 8, 128), f32),
            pltpu.VMEM((8, 4, 8, 128), f32),
            pltpu.VMEM((16, 128), f32),
            pltpu.VMEM((8, 16, 128), f32),
            pltpu.VMEM((8, 16, 128), f32),
            pltpu.VMEM((16, 128), f32),
            pltpu.VMEM((256, 128), jnp.bfloat16),
            pltpu.VMEM((8, 128), f32),
            pltpu.VMEM((1, 128), jnp.int32),
            pltpu.VMEM((1, 64), jnp.int32),
            pltpu.SMEM((1,), jnp.int32),
            pltpu.VMEM((4, 8, 256), f32),
            pltpu.SemaphoreType.DMA((2, 2)),
            pltpu.SemaphoreType.DMA((6,)),
            pltpu.SemaphoreType.DMA((2, 2, 2)),
            pltpu.SemaphoreType.DMA((2, 2, 2)),
            pltpu.SemaphoreType.DMA((8,)),
            pltpu.SemaphoreType.DMA((8,)),
            pltpu.SemaphoreType.DMA((8,)),
            pltpu.SemaphoreType.DMA((8,)),
            pltpu.SemaphoreType.DMA((8,)),
            pltpu.SemaphoreType.DMA((8,)),
            pltpu.SemaphoreType.DMA((8,)),
            pltpu.SemaphoreType.DMA((8,)),
        ],
        compiler_params=pltpu.CompilerParams(
            collective_id=0, has_side_effects=True, vmem_limit_bytes=60 * 1024 * 1024
        ),
    )(source_prev, source_now, adjoint_prev, adjoint_now, squared_courant, offsets, traces, receiver_cells, counts)
    return pl.pallas_call(
        deliver,
        out_shape=tuple(jax.ShapeDtypeStruct(r.shape, f32) for r in results),
        in_specs=[hbm] * 3,
        out_specs=(hbm,) * 3,
        scratch_shapes=[pltpu.VMEM(r.shape, f32) for r in results] + [pltpu.SemaphoreType.DMA((2, 3))],
        compiler_params=pltpu.CompilerParams(vmem_limit_bytes=60 * 1024 * 1024),
    )(*results)


def solution(mesh):
    placed = (
        P("shot", "dom", None, None),
        P("shot", "dom", None, None),
        P("shot", "dom", None, None),
        P("shot", "dom", None, None),
        P("dom", "shot", None),
        P("shot"),
        P("shot", None, "dom"),
        P("shot", None, "dom"),
        P("shot", "dom", None),
    )
    return jax.shard_map(
        shards,
        mesh=mesh,
        in_specs=placed,
        out_specs=(
            P("shot", "dom", None, None),
            P("shot", "dom", None, None),
            P("dom", "shot", None),
        ),
        check_vma=False,
    )
```

```python
import jax
import jax.numpy as jnp
from jax import lax
from jax.experimental import pallas as pl
from jax.experimental.pallas import tpu as pltpu
from jax.sharding import PartitionSpec as P

STEPS = 8
COEFFS = (-205.0 / 72.0, 8.0 / 5.0, -1.0 / 5.0, 8.0 / 315.0, -1.0 / 560.0)
MESH = pl.DeviceIdType.MESH
OWN_ROWS = pl.ds(16, 16)
ALL_ROWS = pl.ds(8, 32)
WAYS = ((1, 0), (-1, 0), (0, 1), (0, -1), (1, 1), (1, -1), (-1, 1), (-1, -1))


def remote(src, dst, send, recv, where):
    return pltpu.make_async_remote_copy(
        src_ref=src, dst_ref=dst, send_sem=send, recv_sem=recv, device_id=where, device_id_type=MESH
    )


def lane_iota(shape):
    return lax.broadcasted_iota(jnp.int32, shape, len(shape) - 1)


def rolled(value, shift):
    return pltpu.roll(value, shift % 128, value.ndim - 1) if shift % 128 else value


def laplace(ref, plane, first, rows):
    center = ref[plane, pl.ds(first, rows)]
    lanes = lane_iota((rows, 128))
    total = 3.0 * COEFFS[0] * center
    for reach in range(1, 5):
        pair = ref[plane + reach, pl.ds(first, rows)] + ref[plane - reach, pl.ds(first, rows)]
        pair = pair + ref[plane, pl.ds(first + reach, rows)] + ref[plane, pl.ds(first - reach, rows)]
        pair = pair + jnp.where(lanes >= reach, rolled(center, reach), 0.0)
        pair = pair + jnp.where(lanes < 128 - reach, rolled(center, -reach), 0.0)
        total = total + COEFFS[reach] * pair
    return center, total


def kernel(
    src_prev, src_now, adj_prev, adj_now, model_in, offsets_in, traces_in, cells_in, counts_in,
    src_out, adj_out, grad_out,
    n, m, cc, courant, image, lap, inj, pieces, grads, trace_send, trace_y, trace_row, slots, tables, onehot,
    traces, cells, counts, offsets, summed, outv,
    small_sem, relay_send, relay_recv, table_send, table_recv, halo_send, halo_recv, side_send, side_recv,
    ty_send, ty_recv, tr_send, tr_recv, c_send, c_recv, g_send, g_recv, o_send, o_recv,
):
    s = lax.axis_index("shot")
    d = lax.axis_index("dom")
    y, g = d // 8, d % 8
    z, c = g // 2, g % 2
    sx, sz = s // 2, s % 2
    xb = 2 * y + c
    hc = z // 2
    home = 2 * y + hc
    place = d % 4
    stays = hc == c

    def block(x_index, z_index):
        return (x_index // 2) * 8 + z_index * 2 + x_index % 2

    def here(shift):
        return y * 8 + ((z + shift) % 4) * 2 + hc

    halves = [
        pltpu.make_async_copy(
            model_in.at[:, :, pl.ds(128 * half, 128)], pieces.at[0, pl.ds(4 * half, 4)], small_sem.at[half]
        )
        for half in range(2)
    ]
    small = [
        pltpu.make_async_copy(ref.at[0], scratch, small_sem.at[2 + i])
        for i, (ref, scratch) in enumerate(((traces_in, traces), (cells_in, cells), (counts_in, counts)))
    ] + [pltpu.make_async_copy(offsets_in, offsets, small_sem.at[5])]
    for copy in small + halves:
        copy.start()

    tables[...] = jnp.zeros((6, 16, 128), jnp.float32)

    def clear_planes(first):
        for f in range(2):
            for plane in range(first, first + 8):
                for par in range(2):
                    n[par, f, plane] = jnp.zeros((48, 128), jnp.float32)
                m[f, plane] = jnp.zeros((48, 128), jnp.float32)
        for plane in range(4):
            cc[(0 if first == 0 else 20) + plane] = jnp.zeros((32, 128), jnp.float32)

    def clear_rows(first):
        for f in range(2):
            for plane in range(32):
                for par in range(2):
                    n[par, f, plane, first : first + 8] = jnp.zeros((8, 128), jnp.float32)
                m[f, plane, first : first + 8] = jnp.zeros((8, 128), jnp.float32)
        for plane in range(24):
            cc[plane, first - 8 : first] = jnp.zeros((8, 128), jnp.float32)

    for ended, clear, first in (
        (xb == 0, clear_planes, 0), (xb == 15, clear_planes, 24), (z == 0, clear_rows, 8), (z == 3, clear_rows, 32)
    ):
        @pl.when(ended)
        def _():
            clear(first)

    barrier = pltpu.get_barrier_semaphore()

    def greet(where):
        pl.semaphore_signal(barrier, inc=1, device_id=where, device_id_type=MESH)

    line = [(s, ((y + k) % 8) * 8 + g) for k in range(1, 8)]
    row = [(s, y * 8 + (g + k) % 8) for k in range(1, 8)]
    shot = {}
    for dz in range(2):
        for k in range(4):
            shot[dz, k] = (((sx + k) % 4) * 2 + (sz + dz) % 2, d)
    others = [key for key in shot if key != (0, 0)]
    for where in line + row + [shot[key] for key in others]:
        greet(where)
    beyond = jnp.where(c == 1, y < 7, y > 0)

    @pl.when(beyond)
    def _():
        for k in range(4):
            greet((s, jnp.where(c == 1, (y + 1) * 8, (y - 1) * 8 + 1) + 2 * k))

    own_gradient = jnp.logical_and(sx == z, stays)
    for k in range(8):
        if k:
            greet(((s + k) % 8, y * 8 + 2 * sx + hc))
        else:
            @pl.when(jnp.logical_not(own_gradient))
            def _():
                greet((s, y * 8 + 2 * sx + hc))

    expected = 21 + 4 * beyond.astype(jnp.int32) + 8 - own_gradient.astype(jnp.int32)
    for copy in small:
        copy.wait()
    off = offsets[0]
    pieces[0, 8] = jnp.full((8, 128), off, jnp.int32).astype(jnp.float32)
    for copy in halves:
        copy.wait()
    pl.semaphore_wait(barrier, expected)

    spread_1 = [
        remote(pieces.at[0], pieces.at[dz * 4 + k], c_send.at[dz * 4 + k], c_recv.at[dz * 4 + k], shot[dz, k])
        for dz, k in ((1, 0), (0, 1), (0, 2), (0, 3))
    ]
    for copy in spread_1:
        copy.start()

    def relay(array, source, target, base, rows, action):
        for k in range(4):
            src = source.at[:, pl.ds(pl.multiple_of(16 * ((z + k) % 4), 16), 16)]
            dst = target.at[pl.ds(base + 4 * place, 4), rows]
            copy = remote(src, dst, relay_send.at[array, k], relay_recv.at[array, place], (s, here(k)))
            if action == "start":
                if k:
                    copy.start()
                else:
                    @pl.when(stays)
                    def _():
                        pltpu.make_async_copy(src, dst, relay_recv.at[array, place]).start()

                    @pl.when(jnp.logical_not(stays))
                    def _():
                        copy.start()
            elif action == "sent":
                if k:
                    copy.wait_send()
                else:
                    @pl.when(jnp.logical_not(stays))
                    def _():
                        copy.wait_send()
            else:
                got = target.at[pl.ds(base + 4 * k, 4), rows]
                remote(got, got, relay_send.at[array, k], relay_recv.at[array, k], (s, here(k))).wait_recv()

    relays = (
        (0, src_now.at[0], n.at[0, 0], 8, OWN_ROWS),
        (1, adj_now.at[0], n.at[0, 1], 8, OWN_ROWS),
        (2, src_prev.at[0], m.at[0], 8, OWN_ROWS),
        (3, adj_prev.at[0], m.at[1], 8, OWN_ROWS),
        (4, courant, cc, 4, pl.ds(8, 16)),
    )
    relay(*relays[0], "start")
    relay(*relays[1], "start")

    def there(way):
        return jnp.logical_and(
            jnp.logical_and(xb + way[0] >= 0, xb + way[0] < 16), jnp.logical_and(z + way[1] >= 0, z + way[1] < 4)
        )

    def parts(way, depth):
        src_plane = {1: 24 - depth, -1: 8, 0: 8}[way[0]]
        dst_plane = {1: 8 - depth, -1: 24, 0: 8}[way[0]]
        planes = depth if way[0] else 16
        src_row = {1: 24, -1: 16, 0: 16}[way[1]]
        dst_row = {1: 8, -1: 32, 0: 16}[way[1]]
        rows = 8 if way[1] else 16
        return src_plane, dst_plane, planes, src_row, dst_row, rows

    def margin(i, target, depth, send, recv, plane_shift=0, row_shift=0):
        sp, dp, planes, sr, dr, rows = parts(WAYS[i], depth)
        return remote(
            target.at[pl.ds(sp - plane_shift, planes), pl.ds(sr - row_shift, rows)],
            target.at[pl.ds(dp - plane_shift, planes), pl.ds(dr - row_shift, rows)],
            send.at[i], recv.at[i], (s, block(xb + WAYS[i][0], z + WAYS[i][1])),
        )

    def halo(i, par, f):
        return margin(i, n.at[par, f], 4 if i >= 4 else 8, halo_send.at[par, f], halo_recv.at[par, f])

    def side(i, which):
        if which == 2:
            return margin(i, cc, 4, side_send.at[2], side_recv.at[2], 4, 8)
        return margin(i, m.at[which], 4, side_send.at[which], side_recv.at[which])

    def each_way(make, count, action):
        for i in range(count):
            if action == "got":
                sender = (-WAYS[i][0], -WAYS[i][1])

                @pl.when(there(sender))
                def _():
                    make(i).wait_recv()
            else:
                @pl.when(there(WAYS[i]))
                def _():
                    if action == "start":
                        make(i).start()
                    else:
                        make(i).wait_send()

    spread = (lax.broadcasted_iota(jnp.int32, (64, 128), 0) == lane_iota((64, 128)) // 2).astype(jnp.float32)
    filled = jnp.broadcast_to(counts[...].astype(jnp.float32), (8, 64))
    live = (lane_iota((8, 128)) % 2).astype(jnp.float32) < jnp.dot(
        filled, spread, preferred_element_type=jnp.float32
    ) - 0.5
    trace_send[0:8] = jnp.where(live, traces[...], 0.0)
    trace_send[8:16] = jnp.broadcast_to(cells[...].astype(jnp.float32), (8, 128))
    first = [
        remote(trace_send, trace_y.at[k], ty_send.at[k], ty_recv.at[k], line[k - 1]) for k in range(1, 8)
    ]
    for copy in first:
        copy.start()
    relay(*relays[2], "start")
    trace_y[0] = trace_send[...]

    spread_1[0].wait_recv()
    spread_2 = [
        remote(pieces.at[4], pieces.at[4 + k], c_send.at[4 + k], c_recv.at[4 + k], shot[0, k]) for k in range(1, 4)
    ]
    for copy in spread_2:
        copy.start()
    for copy in first:
        copy.wait_recv()
    lane = lane_iota((16, 128))
    packed = jnp.zeros((16, 128), jnp.float32)
    for k in range(8):
        packed = packed + jnp.where(lane // 16 == (y + 8 - k) % 8, rolled(trace_y[k], -16 * k), 0.0)
    trace_row[0] = packed
    along = [
        remote(trace_row.at[0], trace_row.at[k], tr_send.at[k], tr_recv.at[k], row[k - 1]) for k in range(1, 8)
    ]
    for copy in along:
        copy.start()

    for f in range(2):
        relay(*relays[f], "got")
        each_way(lambda i: halo(i, 0, f), 8, "start")

    for copy in spread_1[1:] + spread_2:
        copy.wait_recv()
    at = lane_iota((8, 128)) < 128 - off
    turn_back = lax.rem(128 - off, 128)
    for dz in range(2):
        for k in range(4):
            j = ((sx + 4 - k) % 4) * 2 + (sz + dz) % 2
            for plane in range(4):
                low = pltpu.roll(pieces[dz * 4 + k, plane], turn_back, 1)
                high = pltpu.roll(pieces[dz * 4 + k, 4 + plane], turn_back, 1)
                courant[plane, pl.ds(pl.multiple_of(j * 8, 8), 8)] = jnp.where(at, low, high)
    relay(*relays[4], "start")
    relay(*relays[3], "start")

    for copy in along:
        copy.wait_recv()
    own = jnp.zeros((16, 128), jnp.float32)
    for k in range(8):
        own = own + jnp.where((lane // 2) % 8 == (g + 8 - k) % 8, rolled(trace_row[k], -2 * k), 0.0)
    slots[...] = own

    def hand_out(group, x_index, at_place, wanted, action):
        for k in range(4):
            zk = (z + k) % 4
            src, dst = slots, tables.at[at_place]
            copy = remote(src, dst, table_send.at[group, k], table_recv.at[at_place], (s, block(x_index, zk)))
            mine = jnp.logical_and(x_index == xb, zk == z)

            @pl.when(jnp.logical_and(wanted, jnp.logical_not(mine)))
            def _():
                if action == "start":
                    copy.start()
                else:
                    copy.wait_send()

            if action == "start":
                @pl.when(jnp.logical_and(wanted, mine))
                def _():
                    pltpu.make_async_copy(src, dst, table_recv.at[at_place]).start()

    hands = (
        (0, home, 1 + place, home >= 0),
        (1, home + 1, 0, jnp.logical_and(place == 3, home < 15)),
        (2, home - 1, 5, jnp.logical_and(place == 0, home > 0)),
    )
    for hand in hands:
        hand_out(*hand, "start")

    for plane in range(16):
        image[plane] = jnp.zeros((16, 128), jnp.float32)

    relay(*relays[2], "got")
    each_way(lambda i: side(i, 0), 4, "start")
    relay(*relays[4], "got")
    each_way(lambda i: side(i, 2), 4, "start")

    for i in range(6):
        exists = {0: xb > 0, 5: xb < 15}.get(i, xb >= 0)

        @pl.when(exists)
        def _():
            remote(
                tables.at[i], tables.at[i], table_send.at[0, 0], table_recv.at[i], (s, d)
            ).wait_recv()

    for i in range(6):
        cell = tables[i, 8:9].astype(jnp.int32)
        near = ((cell >> 7) & 63) - (16 * z - 8)
        spot = jnp.where(jnp.logical_and(near >= 0, near < 32), (cell >> 13) * 32 + near, -1)
        onehot[i] = (
            lax.broadcasted_iota(jnp.int32, (128, 128), 0) == jnp.broadcast_to(spot, (128, 128))
        ).astype(jnp.float32).astype(jnp.bfloat16)
    relay(*relays[3], "got")
    each_way(lambda i: side(i, 1), 4, "start")
    each_way(lambda i: side(i, 0), 4, "got")
    each_way(lambda i: side(i, 2), 4, "got")
    each_way(lambda i: side(i, 0), 4, "sent")

    dims = (((1,), (1,)), ((), ()))

    def injection(t, kept, places):
        for i in places:
            value = tables[i, pl.ds(t, 1)]
            cell_lane = tables[i, 8:9].astype(jnp.int32) & 127
            hit = lax.broadcasted_iota(jnp.int32, (128, 128), 0) == jnp.broadcast_to(cell_lane, (128, 128))
            put = jnp.where(hit, jnp.broadcast_to(value, (128, 128)), 0.0)
            high = put.astype(jnp.bfloat16)
            low = (put - high.astype(jnp.float32)).astype(jnp.bfloat16)
            inj[kept, 128 * i : 128 * i + 128] = lax.dot_general(
                onehot[i], high, dims, preferred_element_type=jnp.float32
            ) + lax.dot_general(onehot[i], low, dims, preferred_element_type=jnp.float32)

    def step_wide(par, f):
        for quad in (0, 5):
            for i in range(4):
                plane = 4 + 4 * quad + i
                center, total = laplace(n.at[par, f], plane, 16, 16)
                following = 2.0 * center - m[f, plane, OWN_ROWS] + cc[4 * quad + i, 8:24] * total
                if f == 1:
                    following = following + inj[0, 128 * quad + 32 * i + 8 : 128 * quad + 32 * i + 24]
                m[f, plane, OWN_ROWS] = following

        @pl.loop(1, 5)
        def _(quad):
            for i in range(4):
                plane = 4 + 4 * quad + i
                center, total = laplace(n.at[par, f], plane, 8, 32)
                following = 2.0 * center - m[f, plane, ALL_ROWS] + cc[4 * quad + i] * total
                if f == 0:
                    image[plane - 8] += n[par, 1, plane, OWN_ROWS] * total[8:24]
                else:
                    following = following + inj[0, pl.ds(pl.multiple_of(128 * quad + 32 * i, 32), 32)]
                    image[plane - 8] += following[8:24] * lap[plane - 8]
                m[f, plane, ALL_ROWS] = following

    def step_own(par, f):
        @pl.loop(0, 4)
        def _(quad):
            for i in range(4):
                plane = 8 + 4 * quad + i
                center, total = laplace(m.at[f], plane, 16, 16)
                following = 2.0 * center - n[par, f, plane, OWN_ROWS] + cc[4 + 4 * quad + i, 8:24] * total
                if f == 0:
                    lap[plane - 8] = total
                else:
                    following = following + inj[1, pl.ds(pl.multiple_of(128 + 128 * quad + 32 * i + 8, 8), 16)]
                n[1 - par, f, plane, OWN_ROWS] = following

    def give_back(f, action):
        for i in range(4):
            src = n.at[0, f, pl.ds(8 + 4 * i, 4), OWN_ROWS]
            dst = outv.at[f, :, pl.ds(pl.multiple_of(16 * z, 16), 16)]
            copy = remote(src, dst, o_send.at[f, i], o_recv.at[f, z], (s, y * 8 + 4 * c + i))
            mine = g == 4 * c + i

            @pl.when(jnp.logical_not(mine))
            def _():
                if action == "start":
                    copy.start()
                else:
                    copy.wait_send()

            if action == "start":
                @pl.when(mine)
                def _():
                    pltpu.make_async_copy(src, dst, o_recv.at[f, z]).start()

    def turn_image():
        for plane in range(16):
            lap[plane] = pltpu.roll(image[plane] * (1.0 / STEPS), lax.rem(off, 128), 1)

    def send_gradient(action):
        for half in range(2):
            for i in range(4):
                src = lap.at[pl.ds(4 * i, 4), pl.ds(8 * half, 8)]
                dst = grads.at[s]
                to = (2 * z + half, y * 8 + 4 * c + i)
                copy = remote(src, dst, g_send.at[4 * half + i], g_recv.at[s], to)
                mine = jnp.logical_and(s == to[0], d == to[1])

                @pl.when(jnp.logical_not(mine))
                def _():
                    if action == "start":
                        copy.start()
                    else:
                        copy.wait_send()

                if action == "start":
                    @pl.when(mine)
                    def _():
                        pltpu.make_async_copy(src, dst, g_recv.at[s]).start()

    blocks = STEPS // 2

    @pl.loop(0, blocks)
    def _(b):
        par = b % 2
        for f in range(2):
            if f == 1:
                injection(2 * b, 0, range(6))
                injection(2 * b + 1, 1, range(1, 5))

                @pl.when(b == 0)
                def _():
                    each_way(lambda i: side(i, 1), 4, "got")
                    each_way(lambda i: side(i, 1), 4, "sent")

            each_way(lambda i: halo(i, par, f), 8, "got")
            step_wide(par, f)

            @pl.when(b > 0)
            def _():
                each_way(lambda i: halo(i, 1 - par, f), 8, "sent")

            if f == 1:
                @pl.when(b == blocks - 1)
                def _():
                    turn_image()
                    send_gradient("start")

            step_own(par, f)

            @pl.when(b < blocks - 1)
            def _():
                each_way(lambda i: halo(i, 1 - par, f), 8, "start")

            if f == 0:
                @pl.when(b == blocks - 1)
                def _():
                    give_back(0, "start")

    give_back(1, "start")
    results = [
        pltpu.make_async_copy(outv.at[f], ref.at[0], small_sem.at[f]) for f, ref in enumerate((src_out, adj_out))
    ]
    for f in range(2):
        for k in range(4):
            got = outv.at[f, :, pl.ds(16 * k, 16)]
            remote(got, got, o_send.at[f, k], o_recv.at[f, k], (s, d)).wait_recv()
        results[f].start()
    for j in range(8):
        remote(grads.at[j], grads.at[j], g_send.at[j], g_recv.at[j], (s, d)).wait_recv()
    lane8 = lane_iota((8, 128)).astype(jnp.float32)
    for plane in range(4):
        low = jnp.zeros((8, 128), jnp.float32)
        high = jnp.zeros((8, 128), jnp.float32)
        for dz in range(2):
            for k in range(4):
                j = ((sx + 4 - k) % 4) * 2 + (sz + dz) % 2
                part = grads[j, plane]
                start = pieces[dz * 4 + k, 8]
                low = low + jnp.where(lane8 >= start, part, 0.0)
                high = high + jnp.where(lane8 < start, part, 0.0)
        summed[plane, :, 0:128] = low
        summed[plane, :, 128:256] = high
    gradient = pltpu.make_async_copy(summed, grad_out, small_sem.at[2])
    gradient.start()
    for copy in first + along + spread_1 + spread_2:
        copy.wait_send()
    for args in relays:
        relay(*args, "sent")
    for hand in hands:
        hand_out(*hand, "sent")
    each_way(lambda i: side(i, 2), 4, "sent")
    for f in range(2):
        each_way(lambda i: halo(i, 1, f), 8, "sent")
        give_back(f, "sent")
    send_gradient("sent")
    for copy in results + [gradient]:
        copy.wait()


def deliver(*refs):
    given, wanted, held, sems = refs[0:3], refs[3:6], refs[6:9], refs[9]
    into = [pltpu.make_async_copy(a, b, sems.at[0, i]) for i, (a, b) in enumerate(zip(given, held, strict=True))]
    out = [pltpu.make_async_copy(a, b, sems.at[1, i]) for i, (a, b) in enumerate(zip(held, wanted, strict=True))]
    for copy in into:
        copy.start()
    for i in range(3):
        into[i].wait()
        out[i].start()
    for copy in out:
        copy.wait()


def shards(source_prev, source_now, adjoint_prev, adjoint_now, squared_courant, offsets, traces, receiver_cells, counts):
    field = jax.ShapeDtypeStruct(source_now.shape, jnp.float32)
    hbm = pl.BlockSpec(memory_space=pltpu.HBM)
    f32 = jnp.float32
    dma = pltpu.SemaphoreType.DMA
    results = pl.pallas_call(
        kernel,
        out_shape=(field, field, jax.ShapeDtypeStruct(squared_courant.shape, f32)),
        in_specs=[hbm] * 9,
        out_specs=(hbm, hbm, hbm),
        scratch_shapes=[
            pltpu.VMEM((2, 2, 32, 48, 128), f32),
            pltpu.VMEM((2, 32, 48, 128), f32),
            pltpu.VMEM((24, 32, 128), f32),
            pltpu.VMEM((4, 64, 128), f32),
            pltpu.VMEM((16, 16, 128), f32),
            pltpu.VMEM((16, 16, 128), f32),
            pltpu.VMEM((2, 768, 128), f32),
            pltpu.VMEM((8, 9, 8, 128), f32),
            pltpu.VMEM((8, 4, 8, 128), f32),
            pltpu.VMEM((16, 128), f32),
            pltpu.VMEM((8, 16, 128), f32),
            pltpu.VMEM((8, 16, 128), f32),
            pltpu.VMEM((16, 128), f32),
            pltpu.VMEM((6, 16, 128), f32),
            pltpu.VMEM((6, 128, 128), jnp.bfloat16),
            pltpu.VMEM((8, 128), f32),
            pltpu.VMEM((1, 128), jnp.int32),
            pltpu.VMEM((1, 64), jnp.int32),
            pltpu.SMEM((1,), jnp.int32),
            pltpu.VMEM((4, 8, 256), f32),
            pltpu.VMEM((2, 4, 64, 128), f32),
            dma((6,)),
            dma((5, 4)), dma((5, 4)),
            dma((3, 4)), dma((6,)),
            dma((2, 2, 8)), dma((2, 2, 8)),
            dma((3, 4)), dma((3, 4)),
            dma((8,)), dma((8,)), dma((8,)), dma((8,)), dma((8,)), dma((8,)), dma((8,)), dma((8,)),
            dma((2, 4)), dma((2, 4)),
        ],
        compiler_params=pltpu.CompilerParams(
            collective_id=0, has_side_effects=True, vmem_limit_bytes=60 * 1024 * 1024
        ),
    )(source_prev, source_now, adjoint_prev, adjoint_now, squared_courant, offsets, traces, receiver_cells, counts)
    return pl.pallas_call(
        deliver,
        out_shape=tuple(jax.ShapeDtypeStruct(r.shape, f32) for r in results),
        in_specs=[hbm] * 3,
        out_specs=(hbm,) * 3,
        scratch_shapes=[pltpu.VMEM(r.shape, f32) for r in results] + [dma((2, 3))],
        compiler_params=pltpu.CompilerParams(vmem_limit_bytes=60 * 1024 * 1024),
    )(*results)


def solution(mesh):
    placed = (
        P("shot", "dom", None, None),
        P("shot", "dom", None, None),
        P("shot", "dom", None, None),
        P("shot", "dom", None, None),
        P("dom", "shot", None),
        P("shot"),
        P("shot", None, "dom"),
        P("shot", None, "dom"),
        P("shot", "dom", None),
    )
    return jax.shard_map(
        shards,
        mesh=mesh,
        in_specs=placed,
        out_specs=(
            P("shot", "dom", None, None),
            P("shot", "dom", None, None),
            P("dom", "shot", None),
        ),
        check_vma=False,
    )
```

```python
import jax
import jax.numpy as jnp
from jax import lax
from jax.experimental import pallas as pl
from jax.experimental.pallas import tpu as pltpu
from jax.sharding import PartitionSpec as P

STEPS = 8
COEFFS = (-205.0 / 72.0, 8.0 / 5.0, -1.0 / 5.0, 8.0 / 315.0, -1.0 / 560.0)
MESH = pl.DeviceIdType.MESH
OWN_ROWS = pl.ds(16, 16)
ALL_ROWS = pl.ds(8, 32)
WAYS = ((1, 0), (-1, 0), (0, 1), (0, -1), (1, 1), (1, -1), (-1, 1), (-1, -1))


def remote(src, dst, send, recv, where):
    return pltpu.make_async_remote_copy(
        src_ref=src, dst_ref=dst, send_sem=send, recv_sem=recv, device_id=where, device_id_type=MESH
    )


def lane_iota(shape):
    return lax.broadcasted_iota(jnp.int32, shape, len(shape) - 1)


def rolled(value, shift):
    return pltpu.roll(value, shift % 128, value.ndim - 1) if shift % 128 else value


def along_lanes(value, band):
    high = value.astype(jnp.bfloat16)
    low = (value - high.astype(jnp.float32)).astype(jnp.bfloat16)
    return jnp.dot(jnp.concatenate([high, low, high], 1), band[...], preferred_element_type=jnp.float32)


def laplace(ref, plane, first, rows, along):
    center = ref[plane, pl.ds(first, rows)]
    total = 3.0 * COEFFS[0] * center + along
    for reach in range(1, 5):
        pair = ref[plane + reach, pl.ds(first, rows)] + ref[plane - reach, pl.ds(first, rows)]
        pair = pair + ref[plane, pl.ds(first + reach, rows)] + ref[plane, pl.ds(first - reach, rows)]
        total = total + COEFFS[reach] * pair
    return center, total


def kernel(
    src_prev, src_now, adj_prev, adj_now, model_in, offsets_in, traces_in, cells_in, counts_in,
    src_out, adj_out, grad_out,
    n, m, cc, courant, image, lap, inj, pieces, grads, trace_send, trace_y, trace_row, slots, tables, onehot,
    traces, cells, counts, offsets, summed, outv, band, third, offs,
    small_sem, relay_send, relay_recv, table_send, table_recv, halo_send, halo_recv, side_send, side_recv,
    ty_send, ty_recv, tr_send, tr_recv, c_send, c_recv, cr_send, cr_recv, f_send, f_recv, g_send, g_recv, o_send, o_recv,
):
    s = lax.axis_index("shot")
    d = lax.axis_index("dom")
    y, g = d // 8, d % 8
    z, c = g // 2, g % 2
    sx, sz = s // 2, s % 2
    xb = 2 * y + c
    hc = z // 2
    home = 2 * y + hc
    place = d % 4
    stays = hc == c

    def block(x_index, z_index):
        return (x_index // 2) * 8 + z_index * 2 + x_index % 2

    def here(shift):
        return y * 8 + ((z + shift) % 4) * 2 + hc

    halves = [
        pltpu.make_async_copy(
            model_in.at[:, :, pl.ds(128 * half, 128)], pieces.at[0, pl.ds(4 * half, 4)], small_sem.at[half]
        )
        for half in range(2)
    ]
    small = [
        pltpu.make_async_copy(ref.at[0], scratch, small_sem.at[2 + i])
        for i, (ref, scratch) in enumerate(((traces_in, traces), (cells_in, cells), (counts_in, counts)))
    ] + [pltpu.make_async_copy(offsets_in, offsets, small_sem.at[5])]
    for copy in small + halves:
        copy.start()

    tables[...] = jnp.zeros((6, 16, 128), jnp.float32)

    def clear_planes(first):
        for f in range(2):
            for plane in range(first, first + 8):
                for par in range(2):
                    n[par, f, plane] = jnp.zeros((48, 128), jnp.float32)
                m[f, plane] = jnp.zeros((48, 128), jnp.float32)
        for plane in range(4):
            cc[(0 if first == 0 else 20) + plane] = jnp.zeros((32, 128), jnp.float32)

    def clear_rows(first):
        for f in range(2):
            for plane in range(32):
                for par in range(2):
                    n[par, f, plane, first : first + 8] = jnp.zeros((8, 128), jnp.float32)
                m[f, plane, first : first + 8] = jnp.zeros((8, 128), jnp.float32)
        for plane in range(24):
            cc[plane, first - 8 : first] = jnp.zeros((8, 128), jnp.float32)

    for ended, clear, first in (
        (xb == 0, clear_planes, 0), (xb == 15, clear_planes, 24), (z == 0, clear_rows, 8), (z == 3, clear_rows, 32)
    ):
        @pl.when(ended)
        def _():
            clear(first)

    barrier = pltpu.get_barrier_semaphore()

    def greet(where):
        pl.semaphore_signal(barrier, inc=1, device_id=where, device_id_type=MESH)

    line = [(s, ((y + k) % 8) * 8 + g) for k in range(1, 8)]
    row = [(s, y * 8 + (g + k) % 8) for k in range(1, 8)]
    shot = {}
    for dz in range(2):
        for k in range(4):
            shot[dz, k] = (((sx + k) % 4) * 2 + (sz + dz) % 2, d)
    others = [key for key in shot if key != (0, 0)]
    for where in line + row + [shot[key] for key in others]:
        greet(where)
    beyond = jnp.where(c == 1, y < 7, y > 0)

    @pl.when(beyond)
    def _():
        for k in range(4):
            greet((s, jnp.where(c == 1, (y + 1) * 8, (y - 1) * 8 + 1) + 2 * k))

    own_gradient = jnp.logical_and(sx == z, stays)
    for k in range(8):
        if k:
            greet(((s + k) % 8, y * 8 + 2 * sx + hc))
        else:
            @pl.when(jnp.logical_not(own_gradient))
            def _():
                greet((s, y * 8 + 2 * sx + hc))

    for i in range(4):
        greet((2 * sx + 1 - sz, y * 8 + 4 * c + i))
    expected = 25 + 4 * beyond.astype(jnp.int32) + 8 - own_gradient.astype(jnp.int32)
    for copy in small:
        copy.wait()
    off = offsets[0]
    offs[0] = jnp.full((8, 128), off, jnp.int32).astype(jnp.float32)
    for copy in halves:
        copy.wait()
    pl.semaphore_wait(barrier, expected)

    spread_1 = [remote(pieces.at[0], pieces.at[k], c_send.at[k], c_recv.at[k], shot[0, k]) for k in range(1, 4)]
    told = [
        remote(offs.at[0], offs.at[dz * 4 + k], f_send.at[dz * 4 + k], f_recv.at[dz * 4 + k], shot[dz, k])
        for dz, k in others
    ]
    for copy in spread_1 + told:
        copy.start()

    def relay(array, source, target, base, rows, action):
        for k in range(4):
            src = source.at[:, pl.ds(pl.multiple_of(16 * ((z + k) % 4), 16), 16)]
            dst = target.at[pl.ds(base + 4 * place, 4), rows]
            copy = remote(src, dst, relay_send.at[array, k], relay_recv.at[array, place], (s, here(k)))
            if action == "start":
                if k:
                    copy.start()
                else:
                    @pl.when(stays)
                    def _():
                        pltpu.make_async_copy(src, dst, relay_recv.at[array, place]).start()

                    @pl.when(jnp.logical_not(stays))
                    def _():
                        copy.start()
            elif action == "sent":
                if k:
                    copy.wait_send()
                else:
                    @pl.when(jnp.logical_not(stays))
                    def _():
                        copy.wait_send()
            else:
                got = target.at[pl.ds(base + 4 * k, 4), rows]
                remote(got, got, relay_send.at[array, k], relay_recv.at[array, k], (s, here(k))).wait_recv()

    relays = (
        (0, src_now.at[0], n.at[0, 0], 8, OWN_ROWS),
        (1, adj_now.at[0], n.at[0, 1], 8, OWN_ROWS),
        (2, src_prev.at[0], m.at[0], 8, OWN_ROWS),
        (3, adj_prev.at[0], m.at[1], 8, OWN_ROWS),
    )
    relay(*relays[0], "start")
    relay(*relays[1], "start")

    def there(way):
        return jnp.logical_and(
            jnp.logical_and(xb + way[0] >= 0, xb + way[0] < 16), jnp.logical_and(z + way[1] >= 0, z + way[1] < 4)
        )

    def parts(way, depth):
        src_plane = {1: 24 - depth, -1: 8, 0: 8}[way[0]]
        dst_plane = {1: 8 - depth, -1: 24, 0: 8}[way[0]]
        planes = depth if way[0] else 16
        src_row = {1: 24, -1: 16, 0: 16}[way[1]]
        dst_row = {1: 8, -1: 32, 0: 16}[way[1]]
        rows = 8 if way[1] else 16
        return src_plane, dst_plane, planes, src_row, dst_row, rows

    def margin(i, target, depth, send, recv, plane_shift=0, row_shift=0):
        sp, dp, planes, sr, dr, rows = parts(WAYS[i], depth)
        return remote(
            target.at[pl.ds(sp - plane_shift, planes), pl.ds(sr - row_shift, rows)],
            target.at[pl.ds(dp - plane_shift, planes), pl.ds(dr - row_shift, rows)],
            send.at[i], recv.at[i], (s, block(xb + WAYS[i][0], z + WAYS[i][1])),
        )

    def halo(i, par, f):
        return margin(i, n.at[par, f], 4 if i >= 4 else 8, halo_send.at[par, f], halo_recv.at[par, f])

    def side(i, which):
        if which == 2:
            return margin(i, cc, 4, side_send.at[2], side_recv.at[2], 4, 8)
        return margin(i, m.at[which], 4, side_send.at[which], side_recv.at[which])

    def each_way(make, count, action):
        for i in range(count):
            if action == "got":
                sender = (-WAYS[i][0], -WAYS[i][1])

                @pl.when(there(sender))
                def _():
                    make(i).wait_recv()
            else:
                @pl.when(there(WAYS[i]))
                def _():
                    if action == "start":
                        make(i).start()
                    else:
                        make(i).wait_send()

    apart = jnp.abs(lax.broadcasted_iota(jnp.int32, (128, 128), 0) - lane_iota((128, 128)))
    weights = jnp.zeros((128, 128), jnp.float32)
    for reach in range(1, 5):
        weights = jnp.where(apart == reach, COEFFS[reach], weights)
    weights_high = weights.astype(jnp.bfloat16)
    band[0:128] = weights_high
    band[128:256] = weights_high
    band[256:384] = (weights - weights_high.astype(jnp.float32)).astype(jnp.bfloat16)

    spread = (lax.broadcasted_iota(jnp.int32, (64, 128), 0) == lane_iota((64, 128)) // 2).astype(jnp.float32)
    filled = jnp.broadcast_to(counts[...].astype(jnp.float32), (8, 64))
    live = (lane_iota((8, 128)) % 2).astype(jnp.float32) < jnp.dot(
        filled, spread, preferred_element_type=jnp.float32
    ) - 0.5
    trace_send[0:8] = jnp.where(live, traces[...], 0.0)
    trace_send[8:16] = jnp.broadcast_to(cells[...].astype(jnp.float32), (8, 128))
    first = [
        remote(trace_send, trace_y.at[k], ty_send.at[k], ty_recv.at[k], line[k - 1]) for k in range(1, 8)
    ]
    for copy in first:
        copy.start()
    relay(*relays[2], "start")
    trace_y[0] = trace_send[...]

    for copy in spread_1:
        copy.wait_recv()
    for copy in told:
        copy.wait_recv()

    def window(target, tile, shift):
        at = lane_iota((8, 128)).astype(jnp.float32) < 128.0 - tile
        turn_back = lax.rem(128 - shift, 128)
        for k in range(4):
            for plane in range(4):
                low = pltpu.roll(pieces[k, plane], turn_back, 1)
                high = pltpu.roll(pieces[k, 4 + plane], turn_back, 1)
                courant[target, k, plane] = jnp.where(at, low, high)

    def hand_model(target, action):
        for k in range(4):
            rows_at = (sx + 4 - k) % 4
            src = courant.at[target, k]
            dst = cc.at[pl.ds(4 + 4 * place, 4), pl.ds(pl.multiple_of(8 + 8 * sz, 8), 8)]
            where = ((s, 2 * sx + 1 - sz)[target], y * 8 + 2 * rows_at + hc)
            copy = remote(src, dst, cr_send.at[target, k], cr_recv.at[place, sz], where)
            mine = jnp.logical_and(stays, rows_at == z)
            if target:
                if action == "start":
                    copy.start()
                else:
                    copy.wait_send()
                continue

            @pl.when(jnp.logical_not(mine))
            def _():
                if action == "start":
                    copy.start()
                else:
                    copy.wait_send()

            if action == "start":
                @pl.when(mine)
                def _():
                    pltpu.make_async_copy(src, dst, cr_recv.at[place, sz]).start()

    window(1, offs[4], jnp.max(offs[4]).astype(jnp.int32))
    hand_model(1, "start")
    window(0, offs[0], off)
    hand_model(0, "start")

    for copy in first:
        copy.wait_recv()
    lane = lane_iota((16, 128))
    packed = jnp.zeros((16, 128), jnp.float32)
    for k in range(8):
        packed = packed + jnp.where(lane // 16 == (y + 8 - k) % 8, rolled(trace_y[k], -16 * k), 0.0)
    trace_row[0] = packed
    along = [
        remote(trace_row.at[0], trace_row.at[k], tr_send.at[k], tr_recv.at[k], row[k - 1]) for k in range(1, 8)
    ]
    for copy in along:
        copy.start()

    for f in range(2):
        relay(*relays[f], "got")
        each_way(lambda i: halo(i, 0, f), 8, "start")

    relay(*relays[3], "start")

    for copy in along:
        copy.wait_recv()
    own = jnp.zeros((16, 128), jnp.float32)
    for k in range(8):
        own = own + jnp.where((lane // 2) % 8 == (g + 8 - k) % 8, rolled(trace_row[k], -2 * k), 0.0)
    slots[...] = own

    def hand_out(group, x_index, at_place, wanted, action):
        for k in range(4):
            zk = (z + k) % 4
            src, dst = slots, tables.at[at_place]
            copy = remote(src, dst, table_send.at[group, k], table_recv.at[at_place], (s, block(x_index, zk)))
            mine = jnp.logical_and(x_index == xb, zk == z)

            @pl.when(jnp.logical_and(wanted, jnp.logical_not(mine)))
            def _():
                if action == "start":
                    copy.start()
                else:
                    copy.wait_send()

            if action == "start":
                @pl.when(jnp.logical_and(wanted, mine))
                def _():
                    pltpu.make_async_copy(src, dst, table_recv.at[at_place]).start()

    hands = (
        (0, home, 1 + place, home >= 0),
        (1, home + 1, 0, jnp.logical_and(place == 3, home < 15)),
        (2, home - 1, 5, jnp.logical_and(place == 0, home > 0)),
    )
    for hand in hands:
        hand_out(*hand, "start")

    for plane in range(16):
        image[plane] = jnp.zeros((16, 128), jnp.float32)

    relay(*relays[2], "got")
    each_way(lambda i: side(i, 0), 4, "start")
    for p in range(4):
        for half in range(2):
            got = cc.at[pl.ds(4 + 4 * p, 4), pl.ds(8 + 8 * half, 8)]
            remote(got, got, cr_send.at[half, p], cr_recv.at[p, half], (s, d)).wait_recv()
    each_way(lambda i: side(i, 2), 4, "start")

    for i in range(6):
        exists = {0: xb > 0, 5: xb < 15}.get(i, xb >= 0)

        @pl.when(exists)
        def _():
            remote(
                tables.at[i], tables.at[i], table_send.at[0, 0], table_recv.at[i], (s, d)
            ).wait_recv()

    for i in range(6):
        cell = tables[i, 8:9].astype(jnp.int32)
        near = ((cell >> 7) & 63) - (16 * z - 8)
        spot = jnp.where(jnp.logical_and(near >= 0, near < 32), (cell >> 13) * 32 + near, -1)
        onehot[i] = (
            lax.broadcasted_iota(jnp.int32, (128, 128), 0) == jnp.broadcast_to(spot, (128, 128))
        ).astype(jnp.float32).astype(jnp.bfloat16)
    relay(*relays[3], "got")
    each_way(lambda i: side(i, 1), 4, "start")
    each_way(lambda i: side(i, 0), 4, "got")
    each_way(lambda i: side(i, 2), 4, "got")
    each_way(lambda i: side(i, 0), 4, "sent")

    dims = (((1,), (1,)), ((), ()))

    def injection(t, kept, places):
        for i in places:
            value = tables[i, pl.ds(t, 1)]
            cell_lane = tables[i, 8:9].astype(jnp.int32) & 127
            hit = lax.broadcasted_iota(jnp.int32, (128, 128), 0) == jnp.broadcast_to(cell_lane, (128, 128))
            put = jnp.where(hit, jnp.broadcast_to(value, (128, 128)), 0.0)
            high = put.astype(jnp.bfloat16)
            low = (put - high.astype(jnp.float32)).astype(jnp.bfloat16)
            inj[kept, 128 * i : 128 * i + 128] = lax.dot_general(
                onehot[i], high, dims, preferred_element_type=jnp.float32
            ) + lax.dot_general(onehot[i], low, dims, preferred_element_type=jnp.float32)

    def step_wide(par, f):
        for quad in range(6):
            if quad in (0, 5):
                rows, where = OWN_ROWS, pl.ds(128 * quad, 64)
            else:
                rows, where = ALL_ROWS, pl.ds(128 * quad, 128)
            third[where] = along_lanes(n[par, f, pl.ds(4 + 4 * quad, 4), rows].reshape(where.size, 128), band)
        for quad in (0, 5):
            for i in range(4):
                plane = 4 + 4 * quad + i
                center, total = laplace(n.at[par, f], plane, 16, 16, third[128 * quad + 16 * i : 128 * quad + 16 * i + 16])
                following = 2.0 * center - m[f, plane, OWN_ROWS] + cc[4 * quad + i, 8:24] * total
                if f == 1:
                    following = following + inj[0, 128 * quad + 32 * i + 8 : 128 * quad + 32 * i + 24]
                m[f, plane, OWN_ROWS] = following

        @pl.loop(1, 5)
        def _(quad):
            for i in range(4):
                plane = 4 + 4 * quad + i
                along = third[pl.ds(pl.multiple_of(128 * quad + 32 * i, 32), 32)]
                center, total = laplace(n.at[par, f], plane, 8, 32, along)
                following = 2.0 * center - m[f, plane, ALL_ROWS] + cc[4 * quad + i] * total
                if f == 0:
                    image[plane - 8] += n[par, 1, plane, OWN_ROWS] * total[8:24]
                else:
                    following = following + inj[0, pl.ds(pl.multiple_of(128 * quad + 32 * i, 32), 32)]
                    image[plane - 8] += following[8:24] * lap[plane - 8]
                m[f, plane, ALL_ROWS] = following

    def step_own(par, f):
        for quad in range(4):
            third[pl.ds(64 * quad, 64)] = along_lanes(m[f, pl.ds(8 + 4 * quad, 4), OWN_ROWS].reshape(64, 128), band)

        @pl.loop(0, 4)
        def _(quad):
            for i in range(4):
                plane = 8 + 4 * quad + i
                along = third[pl.ds(pl.multiple_of(64 * quad + 16 * i, 16), 16)]
                center, total = laplace(m.at[f], plane, 16, 16, along)
                following = 2.0 * center - n[par, f, plane, OWN_ROWS] + cc[4 + 4 * quad + i, 8:24] * total
                if f == 0:
                    lap[plane - 8] = total
                else:
                    following = following + inj[1, pl.ds(pl.multiple_of(128 + 128 * quad + 32 * i + 8, 8), 16)]
                n[1 - par, f, plane, OWN_ROWS] = following

    def give_back(f, action):
        for i in range(4):
            src = n.at[0, f, pl.ds(8 + 4 * i, 4), OWN_ROWS]
            dst = outv.at[f, :, pl.ds(pl.multiple_of(16 * z, 16), 16)]
            copy = remote(src, dst, o_send.at[f, i], o_recv.at[f, z], (s, y * 8 + 4 * c + i))
            mine = g == 4 * c + i

            @pl.when(jnp.logical_not(mine))
            def _():
                if action == "start":
                    copy.start()
                else:
                    copy.wait_send()

            if action == "start":
                @pl.when(mine)
                def _():
                    pltpu.make_async_copy(src, dst, o_recv.at[f, z]).start()

    def turn_image():
        for plane in range(16):
            lap[plane] = pltpu.roll(image[plane] * (1.0 / STEPS), lax.rem(off, 128), 1)

    def send_gradient(action):
        for half in range(2):
            for i in range(4):
                src = lap.at[pl.ds(4 * i, 4), pl.ds(8 * half, 8)]
                dst = grads.at[s]
                to = (2 * z + half, y * 8 + 4 * c + i)
                copy = remote(src, dst, g_send.at[4 * half + i], g_recv.at[s], to)
                mine = jnp.logical_and(s == to[0], d == to[1])

                @pl.when(jnp.logical_not(mine))
                def _():
                    if action == "start":
                        copy.start()
                    else:
                        copy.wait_send()

                if action == "start":
                    @pl.when(mine)
                    def _():
                        pltpu.make_async_copy(src, dst, g_recv.at[s]).start()

    blocks = STEPS // 2

    @pl.loop(0, blocks)
    def _(b):
        par = b % 2
        for f in range(2):
            if f == 1:
                injection(2 * b, 0, range(6))
                injection(2 * b + 1, 1, range(1, 5))

                @pl.when(b == 0)
                def _():
                    each_way(lambda i: side(i, 1), 4, "got")
                    each_way(lambda i: side(i, 1), 4, "sent")

            each_way(lambda i: halo(i, par, f), 8, "got")
            step_wide(par, f)

            @pl.when(b > 0)
            def _():
                each_way(lambda i: halo(i, 1 - par, f), 8, "sent")

            if f == 1:
                @pl.when(b == blocks - 1)
                def _():
                    turn_image()
                    send_gradient("start")

            step_own(par, f)

            @pl.when(b < blocks - 1)
            def _():
                each_way(lambda i: halo(i, 1 - par, f), 8, "start")

            if f == 0:
                @pl.when(b == blocks - 1)
                def _():
                    give_back(0, "start")

    give_back(1, "start")
    results = [
        pltpu.make_async_copy(outv.at[f], ref.at[0], small_sem.at[f]) for f, ref in enumerate((src_out, adj_out))
    ]
    for f in range(2):
        for k in range(4):
            got = outv.at[f, :, pl.ds(16 * k, 16)]
            remote(got, got, o_send.at[f, k], o_recv.at[f, k], (s, d)).wait_recv()
        results[f].start()
    for j in range(8):
        remote(grads.at[j], grads.at[j], g_send.at[j], g_recv.at[j], (s, d)).wait_recv()
    lane8 = lane_iota((8, 128)).astype(jnp.float32)
    for plane in range(4):
        low = jnp.zeros((8, 128), jnp.float32)
        high = jnp.zeros((8, 128), jnp.float32)
        for dz in range(2):
            for k in range(4):
                j = ((sx + 4 - k) % 4) * 2 + (sz + dz) % 2
                part = grads[j, plane]
                start = offs[dz * 4 + k]
                low = low + jnp.where(lane8 >= start, part, 0.0)
                high = high + jnp.where(lane8 < start, part, 0.0)
        summed[plane, :, 0:128] = low
        summed[plane, :, 128:256] = high
    gradient = pltpu.make_async_copy(summed, grad_out, small_sem.at[2])
    gradient.start()
    for copy in first + along + spread_1 + told:
        copy.wait_send()
    for target in range(2):
        hand_model(target, "sent")
    for args in relays:
        relay(*args, "sent")
    for hand in hands:
        hand_out(*hand, "sent")
    each_way(lambda i: side(i, 2), 4, "sent")
    for f in range(2):
        each_way(lambda i: halo(i, 1, f), 8, "sent")
        give_back(f, "sent")
    send_gradient("sent")
    for copy in results + [gradient]:
        copy.wait()


def deliver(*refs):
    given, wanted, held, sems = refs[0:3], refs[3:6], refs[6:9], refs[9]
    into = [pltpu.make_async_copy(a, b, sems.at[0, i]) for i, (a, b) in enumerate(zip(given, held, strict=True))]
    out = [pltpu.make_async_copy(a, b, sems.at[1, i]) for i, (a, b) in enumerate(zip(held, wanted, strict=True))]
    for copy in into:
        copy.start()
    for i in range(3):
        into[i].wait()
        out[i].start()
    for copy in out:
        copy.wait()


def shards(source_prev, source_now, adjoint_prev, adjoint_now, squared_courant, offsets, traces, receiver_cells, counts):
    field = jax.ShapeDtypeStruct(source_now.shape, jnp.float32)
    hbm = pl.BlockSpec(memory_space=pltpu.HBM)
    f32 = jnp.float32
    dma = pltpu.SemaphoreType.DMA
    results = pl.pallas_call(
        kernel,
        out_shape=(field, field, jax.ShapeDtypeStruct(squared_courant.shape, f32)),
        in_specs=[hbm] * 9,
        out_specs=(hbm, hbm, hbm),
        scratch_shapes=[
            pltpu.VMEM((2, 2, 32, 48, 128), f32),
            pltpu.VMEM((2, 32, 48, 128), f32),
            pltpu.VMEM((24, 32, 128), f32),
            pltpu.VMEM((2, 4, 4, 8, 128), f32),
            pltpu.VMEM((16, 16, 128), f32),
            pltpu.VMEM((16, 16, 128), f32),
            pltpu.VMEM((2, 768, 128), f32),
            pltpu.VMEM((4, 8, 8, 128), f32),
            pltpu.VMEM((8, 4, 8, 128), f32),
            pltpu.VMEM((16, 128), f32),
            pltpu.VMEM((8, 16, 128), f32),
            pltpu.VMEM((8, 16, 128), f32),
            pltpu.VMEM((16, 128), f32),
            pltpu.VMEM((6, 16, 128), f32),
            pltpu.VMEM((6, 128, 128), jnp.bfloat16),
            pltpu.VMEM((8, 128), f32),
            pltpu.VMEM((1, 128), jnp.int32),
            pltpu.VMEM((1, 64), jnp.int32),
            pltpu.SMEM((1,), jnp.int32),
            pltpu.VMEM((4, 8, 256), f32),
            pltpu.VMEM((2, 4, 64, 128), f32),
            pltpu.VMEM((384, 128), jnp.bfloat16),
            pltpu.VMEM((768, 128), f32),
            pltpu.VMEM((8, 8, 128), f32),
            dma((6,)),
            dma((4, 4)), dma((4, 4)),
            dma((3, 4)), dma((6,)),
            dma((2, 2, 8)), dma((2, 2, 8)),
            dma((3, 4)), dma((3, 4)),
            dma((8,)), dma((8,)), dma((8,)), dma((8,)), dma((4,)), dma((4,)), dma((2, 4)), dma((4, 2)),
            dma((8,)), dma((8,)), dma((8,)), dma((8,)),
            dma((2, 4)), dma((2, 4)),
        ],
        compiler_params=pltpu.CompilerParams(
            collective_id=0, has_side_effects=True, vmem_limit_bytes=60 * 1024 * 1024
        ),
    )(source_prev, source_now, adjoint_prev, adjoint_now, squared_courant, offsets, traces, receiver_cells, counts)
    return pl.pallas_call(
        deliver,
        out_shape=tuple(jax.ShapeDtypeStruct(r.shape, f32) for r in results),
        in_specs=[hbm] * 3,
        out_specs=(hbm,) * 3,
        scratch_shapes=[pltpu.VMEM(r.shape, f32) for r in results] + [dma((2, 3))],
        compiler_params=pltpu.CompilerParams(vmem_limit_bytes=60 * 1024 * 1024),
    )(*results)


def solution(mesh):
    placed = (
        P("shot", "dom", None, None),
        P("shot", "dom", None, None),
        P("shot", "dom", None, None),
        P("shot", "dom", None, None),
        P("dom", "shot", None),
        P("shot"),
        P("shot", None, "dom"),
        P("shot", None, "dom"),
        P("shot", "dom", None),
    )
    return jax.shard_map(
        shards,
        mesh=mesh,
        in_specs=placed,
        out_specs=(
            P("shot", "dom", None, None),
            P("shot", "dom", None, None),
            P("dom", "shot", None),
        ),
        check_vma=False,
    )
```

```python
import jax
import jax.numpy as jnp
from jax import lax
from jax.experimental import pallas as pl
from jax.experimental.pallas import tpu as pltpu
from jax.sharding import PartitionSpec as P

STEPS = 8
COEFFS = (-205.0 / 72.0, 8.0 / 5.0, -1.0 / 5.0, 8.0 / 315.0, -1.0 / 560.0)
MESH = pl.DeviceIdType.MESH
OWN_ROWS = pl.ds(16, 16)
ALL_ROWS = pl.ds(8, 32)
WAYS = ((1, 0), (-1, 0), (0, 1), (0, -1), (1, 1), (1, -1), (-1, 1), (-1, -1))


def remote(src, dst, send, recv, where):
    return pltpu.make_async_remote_copy(
        src_ref=src, dst_ref=dst, send_sem=send, recv_sem=recv, device_id=where, device_id_type=MESH
    )


def lane_iota(shape):
    return lax.broadcasted_iota(jnp.int32, shape, len(shape) - 1)


def rolled(value, shift):
    return pltpu.roll(value, shift % 128, value.ndim - 1) if shift % 128 else value


def along_lanes(value, band):
    high = value.astype(jnp.bfloat16)
    low = (value - high.astype(jnp.float32)).astype(jnp.bfloat16)
    return jnp.dot(jnp.concatenate([high, low, high], 1), band[...], preferred_element_type=jnp.float32)


def laplace(ref, plane, first, rows, along):
    center = ref[plane, pl.ds(first, rows)]
    total = 3.0 * COEFFS[0] * center + along
    for reach in range(1, 5):
        pair = ref[plane + reach, pl.ds(first, rows)] + ref[plane - reach, pl.ds(first, rows)]
        pair = pair + ref[plane, pl.ds(first + reach, rows)] + ref[plane, pl.ds(first - reach, rows)]
        total = total + COEFFS[reach] * pair
    return center, total


def kernel(
    src_prev, src_now, adj_prev, adj_now, model_in, offsets_in, traces_in, cells_in, counts_in,
    src_out, adj_out, grad_out,
    n, m, cc, courant, image, lap, inj, pieces, grads, trace_send, trace_y, trace_row, slots, tables, onehot,
    traces, cells, counts, offsets, summed, outv, band, third, offs,
    small_sem, relay_send, relay_recv, table_send, table_recv, halo_send, halo_recv, side_send, side_recv,
    ty_send, ty_recv, tr_send, tr_recv, c_send, c_recv, cr_send, cr_recv, f_send, f_recv, g_send, g_recv, o_send, o_recv,
):
    s = lax.axis_index("shot")
    d = lax.axis_index("dom")
    y, g = d // 8, d % 8
    z, c = g // 2, g % 2
    sx, sz = s // 2, s % 2
    xb = 2 * y + c
    hc = z // 2
    home = 2 * y + hc
    place = d % 4
    stays = hc == c

    def block(x_index, z_index):
        return (x_index // 2) * 8 + z_index * 2 + x_index % 2

    def here(shift):
        return y * 8 + ((z + shift) % 4) * 2 + hc

    halves = [
        pltpu.make_async_copy(
            model_in.at[:, :, pl.ds(128 * half, 128)], pieces.at[0, pl.ds(4 * half, 4)], small_sem.at[half]
        )
        for half in range(2)
    ]
    small = [
        pltpu.make_async_copy(ref.at[0], scratch, small_sem.at[2 + i])
        for i, (ref, scratch) in enumerate(((traces_in, traces), (cells_in, cells), (counts_in, counts)))
    ] + [pltpu.make_async_copy(offsets_in, offsets, small_sem.at[5])]
    for copy in small + halves:
        copy.start()

    tables[...] = jnp.zeros((6, 16, 128), jnp.float32)

    def clear_planes(first):
        for f in range(2):
            for plane in range(first, first + 8):
                for par in range(2):
                    n[par, f, plane] = jnp.zeros((48, 128), jnp.float32)
                m[f, plane] = jnp.zeros((48, 128), jnp.float32)
        for plane in range(4):
            cc[(0 if first == 0 else 20) + plane] = jnp.zeros((32, 128), jnp.float32)

    def clear_rows(first):
        for f in range(2):
            for plane in range(32):
                for par in range(2):
                    n[par, f, plane, first : first + 8] = jnp.zeros((8, 128), jnp.float32)
                m[f, plane, first : first + 8] = jnp.zeros((8, 128), jnp.float32)
        for plane in range(24):
            cc[plane, first - 8 : first] = jnp.zeros((8, 128), jnp.float32)

    for ended, clear, first in (
        (xb == 0, clear_planes, 0), (xb == 15, clear_planes, 24), (z == 0, clear_rows, 8), (z == 3, clear_rows, 32)
    ):
        @pl.when(ended)
        def _():
            clear(first)

    barrier = pltpu.get_barrier_semaphore()

    def greet(where):
        pl.semaphore_signal(barrier, inc=1, device_id=where, device_id_type=MESH)

    line = [(s, ((y + k) % 8) * 8 + g) for k in range(1, 8)]
    row = [(s, y * 8 + (g + k) % 8) for k in range(1, 8)]
    shot = {}
    for dz in range(2):
        for k in range(4):
            shot[dz, k] = (((sx + k) % 4) * 2 + (sz + dz) % 2, d)
    others = [key for key in shot if key != (0, 0)]
    for where in line + row + [shot[key] for key in others]:
        greet(where)
    beyond = jnp.where(c == 1, y < 7, y > 0)

    @pl.when(beyond)
    def _():
        for k in range(4):
            greet((s, jnp.where(c == 1, (y + 1) * 8, (y - 1) * 8 + 1) + 2 * k))

    own_gradient = jnp.logical_and(sx == z, stays)
    for k in range(8):
        if k:
            greet(((s + k) % 8, y * 8 + 2 * sx + hc))
        else:
            @pl.when(jnp.logical_not(own_gradient))
            def _():
                greet((s, y * 8 + 2 * sx + hc))

    for i in range(4):
        greet((2 * sx + 1 - sz, y * 8 + 4 * c + i))
    expected = 25 + 4 * beyond.astype(jnp.int32) + 8 - own_gradient.astype(jnp.int32)
    for copy in small:
        copy.wait()
    off = offsets[0]
    offs[0] = jnp.full((8, 128), off, jnp.int32).astype(jnp.float32)
    for copy in halves:
        copy.wait()
    pl.semaphore_wait(barrier, expected)

    spread_1 = [remote(pieces.at[0], pieces.at[k], c_send.at[k], c_recv.at[k], shot[0, k]) for k in range(1, 4)]
    told = [
        remote(offs.at[0], offs.at[dz * 4 + k], f_send.at[dz * 4 + k], f_recv.at[dz * 4 + k], shot[dz, k])
        for dz, k in others
    ]
    for copy in spread_1 + told:
        copy.start()

    def relay(array, source, target, base, rows, action):
        for k in range(4):
            src = source.at[:, pl.ds(pl.multiple_of(16 * ((z + k) % 4), 16), 16)]
            dst = target.at[pl.ds(base + 4 * place, 4), rows]
            copy = remote(src, dst, relay_send.at[array, k], relay_recv.at[array, place], (s, here(k)))
            if action == "start":
                if k:
                    copy.start()
                else:
                    @pl.when(stays)
                    def _():
                        pltpu.make_async_copy(src, dst, relay_recv.at[array, place]).start()

                    @pl.when(jnp.logical_not(stays))
                    def _():
                        copy.start()
            elif action == "sent":
                if k:
                    copy.wait_send()
                else:
                    @pl.when(jnp.logical_not(stays))
                    def _():
                        copy.wait_send()
            else:
                got = target.at[pl.ds(base + 4 * k, 4), rows]
                remote(got, got, relay_send.at[array, k], relay_recv.at[array, k], (s, here(k))).wait_recv()

    relays = (
        (0, src_now.at[0], n.at[0, 0], 8, OWN_ROWS),
        (1, adj_now.at[0], n.at[0, 1], 8, OWN_ROWS),
        (2, src_prev.at[0], m.at[0], 8, OWN_ROWS),
        (3, adj_prev.at[0], m.at[1], 8, OWN_ROWS),
    )
    relay(*relays[0], "start")
    relay(*relays[1], "start")

    def there(way):
        return jnp.logical_and(
            jnp.logical_and(xb + way[0] >= 0, xb + way[0] < 16), jnp.logical_and(z + way[1] >= 0, z + way[1] < 4)
        )

    def parts(way, depth):
        src_plane = {1: 24 - depth, -1: 8, 0: 8}[way[0]]
        dst_plane = {1: 8 - depth, -1: 24, 0: 8}[way[0]]
        planes = depth if way[0] else 16
        src_row = {1: 24, -1: 16, 0: 16}[way[1]]
        dst_row = {1: 8, -1: 32, 0: 16}[way[1]]
        rows = 8 if way[1] else 16
        return src_plane, dst_plane, planes, src_row, dst_row, rows

    def margin(i, target, depth, send, recv, plane_shift=0, row_shift=0):
        sp, dp, planes, sr, dr, rows = parts(WAYS[i], depth)
        return remote(
            target.at[pl.ds(sp - plane_shift, planes), pl.ds(sr - row_shift, rows)],
            target.at[pl.ds(dp - plane_shift, planes), pl.ds(dr - row_shift, rows)],
            send.at[i], recv.at[i], (s, block(xb + WAYS[i][0], z + WAYS[i][1])),
        )

    def halo(i, par, f):
        return margin(i, n.at[par, f], 4 if i >= 4 else 8, halo_send.at[par, f], halo_recv.at[par, f])

    def side(i, which):
        if which == 2:
            return margin(i, cc, 4, side_send.at[2], side_recv.at[2], 4, 8)
        return margin(i, m.at[which], 4, side_send.at[which], side_recv.at[which])

    def each_way(make, count, action):
        for i in range(count):
            if action == "got":
                sender = (-WAYS[i][0], -WAYS[i][1])

                @pl.when(there(sender))
                def _():
                    make(i).wait_recv()
            else:
                @pl.when(there(WAYS[i]))
                def _():
                    if action == "start":
                        make(i).start()
                    else:
                        make(i).wait_send()

    apart = jnp.abs(lax.broadcasted_iota(jnp.int32, (128, 128), 0) - lane_iota((128, 128)))
    weights = jnp.zeros((128, 128), jnp.float32)
    for reach in range(1, 5):
        weights = jnp.where(apart == reach, COEFFS[reach], weights)
    weights_high = weights.astype(jnp.bfloat16)
    band[0:128] = weights_high
    band[128:256] = weights_high
    band[256:384] = (weights - weights_high.astype(jnp.float32)).astype(jnp.bfloat16)

    spread = (lax.broadcasted_iota(jnp.int32, (64, 128), 0) == lane_iota((64, 128)) // 2).astype(jnp.float32)
    filled = jnp.broadcast_to(counts[...].astype(jnp.float32), (8, 64))
    live = (lane_iota((8, 128)) % 2).astype(jnp.float32) < jnp.dot(
        filled, spread, preferred_element_type=jnp.float32
    ) - 0.5
    trace_send[0:8] = jnp.where(live, traces[...], 0.0)
    trace_send[8:16] = jnp.broadcast_to(cells[...].astype(jnp.float32), (8, 128))
    first = [
        remote(trace_send, trace_y.at[k], ty_send.at[k], ty_recv.at[k], line[k - 1]) for k in range(1, 8)
    ]
    for copy in first:
        copy.start()
    relay(*relays[2], "start")
    trace_y[0] = trace_send[...]

    for copy in spread_1:
        copy.wait_recv()
    for copy in told:
        copy.wait_recv()

    def window(target, tile, shift):
        at = lane_iota((8, 128)).astype(jnp.float32) < 128.0 - tile
        turn_back = lax.rem(128 - shift, 128)
        for k in range(4):
            for plane in range(4):
                low = pltpu.roll(pieces[k, plane], turn_back, 1)
                high = pltpu.roll(pieces[k, 4 + plane], turn_back, 1)
                courant[target, k, plane] = jnp.where(at, low, high)

    def hand_model(target, action):
        for k in range(4):
            rows_at = (sx + 4 - k) % 4
            src = courant.at[target, k]
            dst = cc.at[pl.ds(4 + 4 * place, 4), pl.ds(pl.multiple_of(8 + 8 * sz, 8), 8)]
            where = ((s, 2 * sx + 1 - sz)[target], y * 8 + 2 * rows_at + hc)
            copy = remote(src, dst, cr_send.at[target, k], cr_recv.at[place, sz], where)
            mine = jnp.logical_and(stays, rows_at == z)
            if target:
                if action == "start":
                    copy.start()
                else:
                    copy.wait_send()
                continue

            @pl.when(jnp.logical_not(mine))
            def _():
                if action == "start":
                    copy.start()
                else:
                    copy.wait_send()

            if action == "start":
                @pl.when(mine)
                def _():
                    pltpu.make_async_copy(src, dst, cr_recv.at[place, sz]).start()

    window(1, offs[4], jnp.max(offs[4]).astype(jnp.int32))
    hand_model(1, "start")
    window(0, offs[0], off)
    hand_model(0, "start")

    for copy in first:
        copy.wait_recv()
    lane = lane_iota((16, 128))
    packed = jnp.zeros((16, 128), jnp.float32)
    for k in range(8):
        packed = packed + jnp.where(lane // 16 == (y + 8 - k) % 8, rolled(trace_y[k], -16 * k), 0.0)
    trace_row[0] = packed
    along = [
        remote(trace_row.at[0], trace_row.at[k], tr_send.at[k], tr_recv.at[k], row[k - 1]) for k in range(1, 8)
    ]
    for copy in along:
        copy.start()

    for f in range(2):
        relay(*relays[f], "got")
        each_way(lambda i: halo(i, 0, f), 8, "start")

    relay(*relays[3], "start")

    for copy in along:
        copy.wait_recv()
    own = jnp.zeros((16, 128), jnp.float32)
    for k in range(8):
        own = own + jnp.where((lane // 2) % 8 == (g + 8 - k) % 8, rolled(trace_row[k], -2 * k), 0.0)
    slots[...] = own

    def hand_out(group, x_index, at_place, wanted, action):
        for k in range(4):
            zk = (z + k) % 4
            src, dst = slots, tables.at[at_place]
            copy = remote(src, dst, table_send.at[group, k], table_recv.at[at_place], (s, block(x_index, zk)))
            mine = jnp.logical_and(x_index == xb, zk == z)

            @pl.when(jnp.logical_and(wanted, jnp.logical_not(mine)))
            def _():
                if action == "start":
                    copy.start()
                else:
                    copy.wait_send()

            if action == "start":
                @pl.when(jnp.logical_and(wanted, mine))
                def _():
                    pltpu.make_async_copy(src, dst, table_recv.at[at_place]).start()

    hands = (
        (0, home, 1 + place, home >= 0),
        (1, home + 1, 0, jnp.logical_and(place == 3, home < 15)),
        (2, home - 1, 5, jnp.logical_and(place == 0, home > 0)),
    )
    for hand in hands:
        hand_out(*hand, "start")

    for plane in range(16):
        image[plane] = jnp.zeros((16, 128), jnp.float32)

    relay(*relays[2], "got")
    each_way(lambda i: side(i, 0), 4, "start")
    for p in range(4):
        for half in range(2):
            got = cc.at[pl.ds(4 + 4 * p, 4), pl.ds(8 + 8 * half, 8)]
            remote(got, got, cr_send.at[half, p], cr_recv.at[p, half], (s, d)).wait_recv()
    each_way(lambda i: side(i, 2), 4, "start")

    for i in range(6):
        exists = {0: xb > 0, 5: xb < 15}.get(i, xb >= 0)

        @pl.when(exists)
        def _():
            remote(
                tables.at[i], tables.at[i], table_send.at[0, 0], table_recv.at[i], (s, d)
            ).wait_recv()

    for i in range(6):
        cell = tables[i, 8:9].astype(jnp.int32)
        near = ((cell >> 7) & 63) - (16 * z - 8)
        spot = jnp.where(jnp.logical_and(near >= 0, near < 32), (cell >> 13) * 32 + near, -1)
        onehot[i] = (
            lax.broadcasted_iota(jnp.int32, (128, 128), 0) == jnp.broadcast_to(spot, (128, 128))
        ).astype(jnp.float32).astype(jnp.bfloat16)
    relay(*relays[3], "got")
    each_way(lambda i: side(i, 1), 4, "start")
    each_way(lambda i: side(i, 0), 4, "got")
    each_way(lambda i: side(i, 2), 4, "got")
    each_way(lambda i: side(i, 0), 4, "sent")

    dims = (((1,), (1,)), ((), ()))

    def injection(t, kept, places):
        for i in places:
            value = tables[i, pl.ds(t, 1)]
            cell_lane = tables[i, 8:9].astype(jnp.int32) & 127
            hit = lax.broadcasted_iota(jnp.int32, (128, 128), 0) == jnp.broadcast_to(cell_lane, (128, 128))
            put = jnp.where(hit, jnp.broadcast_to(value, (128, 128)), 0.0)
            high = put.astype(jnp.bfloat16)
            low = (put - high.astype(jnp.float32)).astype(jnp.bfloat16)
            inj[kept, 128 * i : 128 * i + 128] = lax.dot_general(
                onehot[i], high, dims, preferred_element_type=jnp.float32
            ) + lax.dot_general(onehot[i], low, dims, preferred_element_type=jnp.float32)

    def step_wide(par, f):
        for quad in range(6):
            if quad in (0, 5):
                rows, where = OWN_ROWS, pl.ds(128 * quad, 64)
            else:
                rows, where = ALL_ROWS, pl.ds(128 * quad, 128)
            third[where] = along_lanes(n[par, f, pl.ds(4 + 4 * quad, 4), rows].reshape(where.size, 128), band)
        for quad in (0, 5):
            for i in range(4):
                plane = 4 + 4 * quad + i
                center, total = laplace(n.at[par, f], plane, 16, 16, third[128 * quad + 16 * i : 128 * quad + 16 * i + 16])
                following = 2.0 * center - m[f, plane, OWN_ROWS] + cc[4 * quad + i, 8:24] * total
                if f == 1:
                    following = following + inj[0, 128 * quad + 32 * i + 8 : 128 * quad + 32 * i + 24]
                m[f, plane, OWN_ROWS] = following

        @pl.loop(1, 5)
        def _(quad):
            for i in range(4):
                plane = 4 + 4 * quad + i
                along = third[pl.ds(pl.multiple_of(128 * quad + 32 * i, 32), 32)]
                center, total = laplace(n.at[par, f], plane, 8, 32, along)
                following = 2.0 * center - m[f, plane, ALL_ROWS] + cc[4 * quad + i] * total
                if f == 0:
                    image[plane - 8] += n[par, 1, plane, OWN_ROWS] * total[8:24]
                else:
                    following = following + inj[0, pl.ds(pl.multiple_of(128 * quad + 32 * i, 32), 32)]
                    image[plane - 8] += following[8:24] * lap[plane - 8]
                m[f, plane, ALL_ROWS] = following

    def give_part(f, i, action):
        src = n.at[0, f, pl.ds(8 + 4 * i, 4), OWN_ROWS]
        dst = outv.at[f, :, pl.ds(pl.multiple_of(16 * z, 16), 16)]
        copy = remote(src, dst, o_send.at[f, i], o_recv.at[f, z], (s, y * 8 + 4 * c + i))
        mine = g == 4 * c + i

        @pl.when(jnp.logical_not(mine))
        def _():
            if action == "start":
                copy.start()
            else:
                copy.wait_send()

        if action == "start":
            @pl.when(mine)
            def _():
                pltpu.make_async_copy(src, dst, o_recv.at[f, z]).start()

    def step_own(par, f, last):
        for quad in range(4):
            third[pl.ds(64 * quad, 64)] = along_lanes(m[f, pl.ds(8 + 4 * quad, 4), OWN_ROWS].reshape(64, 128), band)

        @pl.loop(0, 4)
        def _(quad):
            for i in range(4):
                plane = 8 + 4 * quad + i
                along = third[pl.ds(pl.multiple_of(64 * quad + 16 * i, 16), 16)]
                center, total = laplace(m.at[f], plane, 16, 16, along)
                following = 2.0 * center - n[par, f, plane, OWN_ROWS] + cc[4 + 4 * quad + i, 8:24] * total
                if f == 0:
                    lap[plane - 8] = total
                else:
                    following = following + inj[1, pl.ds(pl.multiple_of(128 + 128 * quad + 32 * i + 8, 8), 16)]
                n[1 - par, f, plane, OWN_ROWS] = following

            @pl.when(last)
            def _():
                give_part(f, quad, "start")

    def turn_image():
        for plane in range(16):
            lap[plane] = pltpu.roll(image[plane] * (1.0 / STEPS), lax.rem(off, 128), 1)

    def send_gradient(action):
        for half in range(2):
            for i in range(4):
                src = lap.at[pl.ds(4 * i, 4), pl.ds(8 * half, 8)]
                dst = grads.at[s]
                to = (2 * z + half, y * 8 + 4 * c + i)
                copy = remote(src, dst, g_send.at[4 * half + i], g_recv.at[s], to)
                mine = jnp.logical_and(s == to[0], d == to[1])

                @pl.when(jnp.logical_not(mine))
                def _():
                    if action == "start":
                        copy.start()
                    else:
                        copy.wait_send()

                if action == "start":
                    @pl.when(mine)
                    def _():
                        pltpu.make_async_copy(src, dst, g_recv.at[s]).start()

    blocks = STEPS // 2

    @pl.loop(0, blocks)
    def _(b):
        par = b % 2
        for f in range(2):
            if f == 1:
                injection(2 * b, 0, range(6))
                injection(2 * b + 1, 1, range(1, 5))

                @pl.when(b == 0)
                def _():
                    each_way(lambda i: side(i, 1), 4, "got")
                    each_way(lambda i: side(i, 1), 4, "sent")

            each_way(lambda i: halo(i, par, f), 8, "got")
            step_wide(par, f)

            @pl.when(b > 0)
            def _():
                each_way(lambda i: halo(i, 1 - par, f), 8, "sent")

            if f == 1:
                @pl.when(b == blocks - 1)
                def _():
                    turn_image()
                    send_gradient("start")

            step_own(par, f, b == blocks - 1)

            @pl.when(b < blocks - 1)
            def _():
                each_way(lambda i: halo(i, 1 - par, f), 8, "start")


    results = [
        pltpu.make_async_copy(outv.at[f], ref.at[0], small_sem.at[f]) for f, ref in enumerate((src_out, adj_out))
    ]
    for f in range(2):
        for k in range(4):
            got = outv.at[f, :, pl.ds(16 * k, 16)]
            remote(got, got, o_send.at[f, k], o_recv.at[f, k], (s, d)).wait_recv()
        results[f].start()
    for j in range(8):
        remote(grads.at[j], grads.at[j], g_send.at[j], g_recv.at[j], (s, d)).wait_recv()
    lane8 = lane_iota((8, 128)).astype(jnp.float32)
    for plane in range(4):
        low = jnp.zeros((8, 128), jnp.float32)
        high = jnp.zeros((8, 128), jnp.float32)
        for dz in range(2):
            for k in range(4):
                j = ((sx + 4 - k) % 4) * 2 + (sz + dz) % 2
                part = grads[j, plane]
                start = offs[dz * 4 + k]
                low = low + jnp.where(lane8 >= start, part, 0.0)
                high = high + jnp.where(lane8 < start, part, 0.0)
        summed[plane, :, 0:128] = low
        summed[plane, :, 128:256] = high
    gradient = pltpu.make_async_copy(summed, grad_out, small_sem.at[2])
    gradient.start()
    for copy in first + along + spread_1 + told:
        copy.wait_send()
    for target in range(2):
        hand_model(target, "sent")
    for args in relays:
        relay(*args, "sent")
    for hand in hands:
        hand_out(*hand, "sent")
    each_way(lambda i: side(i, 2), 4, "sent")
    for f in range(2):
        each_way(lambda i: halo(i, 1, f), 8, "sent")
        for i in range(4):
            give_part(f, i, "sent")
    send_gradient("sent")
    for copy in results + [gradient]:
        copy.wait()


def deliver(*refs):
    given, wanted, held, sems = refs[0:3], refs[3:6], refs[6:9], refs[9]
    into = [pltpu.make_async_copy(a, b, sems.at[0, i]) for i, (a, b) in enumerate(zip(given, held, strict=True))]
    out = [pltpu.make_async_copy(a, b, sems.at[1, i]) for i, (a, b) in enumerate(zip(held, wanted, strict=True))]
    for copy in into:
        copy.start()
    for i in range(3):
        into[i].wait()
        out[i].start()
    for copy in out:
        copy.wait()


def shards(source_prev, source_now, adjoint_prev, adjoint_now, squared_courant, offsets, traces, receiver_cells, counts):
    field = jax.ShapeDtypeStruct(source_now.shape, jnp.float32)
    hbm = pl.BlockSpec(memory_space=pltpu.HBM)
    f32 = jnp.float32
    dma = pltpu.SemaphoreType.DMA
    results = pl.pallas_call(
        kernel,
        out_shape=(field, field, jax.ShapeDtypeStruct(squared_courant.shape, f32)),
        in_specs=[hbm] * 9,
        out_specs=(hbm, hbm, hbm),
        scratch_shapes=[
            pltpu.VMEM((2, 2, 32, 48, 128), f32),
            pltpu.VMEM((2, 32, 48, 128), f32),
            pltpu.VMEM((24, 32, 128), f32),
            pltpu.VMEM((2, 4, 4, 8, 128), f32),
            pltpu.VMEM((16, 16, 128), f32),
            pltpu.VMEM((16, 16, 128), f32),
            pltpu.VMEM((2, 768, 128), f32),
            pltpu.VMEM((4, 8, 8, 128), f32),
            pltpu.VMEM((8, 4, 8, 128), f32),
            pltpu.VMEM((16, 128), f32),
            pltpu.VMEM((8, 16, 128), f32),
            pltpu.VMEM((8, 16, 128), f32),
            pltpu.VMEM((16, 128), f32),
            pltpu.VMEM((6, 16, 128), f32),
            pltpu.VMEM((6, 128, 128), jnp.bfloat16),
            pltpu.VMEM((8, 128), f32),
            pltpu.VMEM((1, 128), jnp.int32),
            pltpu.VMEM((1, 64), jnp.int32),
            pltpu.SMEM((1,), jnp.int32),
            pltpu.VMEM((4, 8, 256), f32),
            pltpu.VMEM((2, 4, 64, 128), f32),
            pltpu.VMEM((384, 128), jnp.bfloat16),
            pltpu.VMEM((768, 128), f32),
            pltpu.VMEM((8, 8, 128), f32),
            dma((6,)),
            dma((4, 4)), dma((4, 4)),
            dma((3, 4)), dma((6,)),
            dma((2, 2, 8)), dma((2, 2, 8)),
            dma((3, 4)), dma((3, 4)),
            dma((8,)), dma((8,)), dma((8,)), dma((8,)), dma((4,)), dma((4,)), dma((2, 4)), dma((4, 2)),
            dma((8,)), dma((8,)), dma((8,)), dma((8,)),
            dma((2, 4)), dma((2, 4)),
        ],
        compiler_params=pltpu.CompilerParams(
            collective_id=0, has_side_effects=True, vmem_limit_bytes=60 * 1024 * 1024
        ),
    )(source_prev, source_now, adjoint_prev, adjoint_now, squared_courant, offsets, traces, receiver_cells, counts)
    return pl.pallas_call(
        deliver,
        out_shape=tuple(jax.ShapeDtypeStruct(r.shape, f32) for r in results),
        in_specs=[hbm] * 3,
        out_specs=(hbm,) * 3,
        scratch_shapes=[pltpu.VMEM(r.shape, f32) for r in results] + [dma((2, 3))],
        compiler_params=pltpu.CompilerParams(vmem_limit_bytes=60 * 1024 * 1024),
    )(*results)


def solution(mesh):
    placed = (
        P("shot", "dom", None, None),
        P("shot", "dom", None, None),
        P("shot", "dom", None, None),
        P("shot", "dom", None, None),
        P("dom", "shot", None),
        P("shot"),
        P("shot", None, "dom"),
        P("shot", None, "dom"),
        P("shot", "dom", None),
    )
    return jax.shard_map(
        shards,
        mesh=mesh,
        in_specs=placed,
        out_specs=(
            P("shot", "dom", None, None),
            P("shot", "dom", None, None),
            P("dom", "shot", None),
        ),
        check_vma=False,
    )
```
